256 devices in a mesh: group: 8 (over z), dev: 32 (over y, x, core).
Axes of the slice: x: 4, y: 4, z: 8, core: 2. Of those that a mesh axis runs over, the one named last changes fastest.
Arguments:
- fine_state: float32 [5, 256, 65536], P(None, 'group', 'dev'), may hold values from -2 to 9.25, as said below
- coarse_boxes: float32 [32768, 5, 512], P(('group', 'dev')), may hold values from -2 to 9.25, as said below
- piece_owner: int32 [8192, 1], P(('group', 'dev')), may hold values from 0 to 31; in each aligned block of 32 rows (0 to 31, 32 to 63, ...) at most 4 rows name the same one
- piece_box: int32 [8192], P(('group', 'dev')), may hold values from 0 to 127
Outputs:
- fine_next: float32 [5, 256, 65536], P(None, 'group', 'dev')
- flux_register: float32 [5, 32, 32768], P(None, None, ('group', 'dev'))
The draws below stay inside these ranges and needn't reach their ends.
Inputs may be any that keep to these rules, and one draw needn't show every extreme that they name: `piece_owner`: among the pieces of one device no owner is named more than 4 times, and in some devices one owner is named exactly 4 times. `fine_state`: conserved variables of states with density in 0.5 to 2, velocity components in -1 to 1 and pressure in 0.4 to 2.5. `coarse_boxes`: conserved variables of states with density in 0.5 to 2, velocity components in -1 to 1 and pressure in 0.4 to 2.5.
All inputs are finite; a program needn't handle non-finite values.
Results may differ from the reference program's by a relative error of at most 0.0003.
Values sent between devices are 32-bit elements; how exact they have to be, the bound alone decides.
A program may use at most 128 MiB of HBM per device.

```python
import math
import jax
import jax.numpy as jnp
import numpy as np
from jax import lax

PS = 16
RATIO = 4
QS = 16
PATCH_Y = 2
PATCH_X = 8
BOX_DEV = 128
CF = 4
CB = 8
PIECE_DEV = 32
MOST = 4
NXF = 4096
NYF = 256
PIECES = 8192
NBOX = 32768
N_GROUP = 8
N_DEV = 32
DEVICES = 256


def gas_sample(key, cells_shape):
    subkeys = jax.random.split(key, 5)
    density = jnp.exp(jax.random.uniform(subkeys[0], cells_shape, jnp.float32, math.log(0.5), math.log(2.0)))
    pressure = jnp.exp(jax.random.uniform(subkeys[4], cells_shape, jnp.float32, math.log(0.4), math.log(2.5)))
    density = jnp.clip(density, 0.5, 2.0)
    pressure = jnp.clip(pressure, 0.4, 2.5)
    velocity = [jax.random.uniform(subkeys[1 + number], cells_shape, jnp.float32, -1.0, 1.0) for number in range(3)]
    energy = pressure / 0.4 + 0.5 * density * (velocity[0] * velocity[0] + velocity[1] * velocity[1] + velocity[2] * velocity[2])
    return jnp.stack([density, density * velocity[0], density * velocity[1], density * velocity[2], energy])


def draw_fine_state(key, part):
    return gas_sample(jax.random.fold_in(key, 11), (NYF, NXF * PS)).astype(jnp.float32)


def draw_coarse_boxes(key, part):
    cells = gas_sample(jax.random.fold_in(key, 23), (NBOX, CB * CB * CB))
    return cells.transpose(1, 0, 2).astype(jnp.float32)


def plant(values, stream_key, least, high):
    longest = values.shape.index(max(values.shape))
    spots = []
    for shift in (0, 1):
        where = [jax.random.randint(jax.random.fold_in(stream_key, axis), (), 0, length) for axis, length in enumerate(values.shape)]
        where[longest] = (where[longest] + shift) % values.shape[longest]
        spots.append(tuple(where))
    return values.at[spots[0]].set(least).at[spots[1]].set(high)


def routed_block(rng, own, number, rows, amount, top, reach, lean):
    sequence = jax.random.permutation(rng, amount)
    crowded, usual = shares(amount, rows * top, reach, lean, True), shares(amount, rows * top, reach, lean, False)
    places = jnp.arange(amount)

    def named(tallies, turn):
        used = int((tallies > 0).sum())
        fixed = max(1, used // 4)
        moved = fixed + (places - fixed + turn * (used - fixed)) % max(1, amount - fixed)
        return jnp.zeros((amount,), jnp.int32).at[sequence[jnp.where(places < fixed, places, moved)]].set(jnp.asarray(tallies, jnp.int32))

    tallies = jnp.where(number % 4 == 0, named(crowded, number // 4), named(usual, number - number // 4 - 1))
    mixed = jax.random.permutation(jax.random.fold_in(own, 3), amount)
    source_of, sink = mixed[0:amount // 2 * 2:2], mixed[1:amount // 2 * 2:2]
    margin = jnp.minimum(tallies[source_of] - 1, reach - tallies[sink]) // 2
    margin = jnp.where((source_of == sequence[0]) | (sink == sequence[0]) | (tallies[sink] == 0), 0, jnp.maximum(margin, 0))
    moved = jax.random.randint(jax.random.fold_in(own, 4), (amount // 2,), 0, 1 << 20) % (margin + 1)
    tallies = tallies.at[source_of].add(-moved).at[sink].add(moved)
    members = jnp.searchsorted(jnp.cumsum(tallies), jnp.arange(rows * top), side="right").astype(jnp.int32)
    table = members.reshape(top, rows).T
    table = table[jax.random.permutation(jax.random.fold_in(own, 1), rows)]
    turn = jax.random.randint(jax.random.fold_in(own, 2), (rows, 1), 0, top)
    return jnp.take_along_axis(table, (jnp.arange(top)[None, :] + turn) % top, axis=1)


def shares(amount, total, reach, skew, full):
    weights = [(1 << 20) // math.isqrt(rank ** skew) + 1 for rank in range(1, amount + 1)]
    largest = reach if full else min(reach, max(-(-total // amount), total * weights[0] // sum(weights)))
    least = 1 if total - largest >= amount - 1 else 0
    given, spare = [largest] + [least] * (amount - 1), total - largest - least * (amount - 1)
    while spare > 0:
        free = [i for i in range(1, amount) if given[i] < largest] or [i for i in range(1, amount) if given[i] < reach]
        pool, remaining = sum([weights[i] for i in free]), spare
        for i in free:
            more = min(reach - given[i], max(1, remaining * weights[i] // pool), spare)
            given[i] = given[i] + more
            spare = spare - more
    return np.array(given)


def setup_inputs(seed: int = 0) -> dict:
    splits = jax.random.split(jax.random.key(seed), 5)
    fine_state = draw_fine_state(jax.random.fold_in(splits[4], 71), 0)
    coarse_boxes = draw_coarse_boxes(jax.random.fold_in(splits[4], 71), 0)
    piece_owner_keys = jax.random.split(jax.random.fold_in(splits[2], 1), PIECES // PIECE_DEV)
    piece_owner_turns = jax.random.permutation(jax.random.fold_in(splits[2], 3), PIECES // PIECE_DEV)
    piece_owner = jax.vmap(lambda own, number: routed_block(jax.random.fold_in(splits[2], 2), own, number, PIECE_DEV, N_DEV, 1, MOST, 2))(piece_owner_keys, piece_owner_turns).reshape((PIECES, 1))
    piece_box = plant(jax.random.randint(splits[3], (PIECES,), 0, BOX_DEV), jax.random.fold_in(splits[3], 1), 0, BOX_DEV - 1).astype(jnp.int32)
    return dict(fine_state=fine_state, coarse_boxes=coarse_boxes, piece_owner=piece_owner, piece_box=piece_box)


GAMMA = 1.4
DT_DX = 0.08

def minmod(lower_diff, upper_diff):
    return jnp.where(lower_diff * upper_diff > 0.0, jnp.where(jnp.abs(lower_diff) < jnp.abs(upper_diff), lower_diff, upper_diff), 0.0)

def to_primitive(conserved):
    density = conserved[0]
    momentum = conserved[1:4]
    kinetic = 0.5 * (momentum[0] * momentum[0] + momentum[1] * momentum[1] + momentum[2] * momentum[2]) / density
    pressure = (GAMMA - 1.0) * (conserved[4] - kinetic)
    return jnp.stack([density, momentum[0] / density, momentum[1] / density, momentum[2] / density, pressure])

def state_terms(primitive, normal):
    density = primitive[0]
    pressure = primitive[4]
    normal_speed = primitive[1 + normal]
    energy = pressure / (GAMMA - 1.0) + 0.5 * density * (primitive[1] * primitive[1] + primitive[2] * primitive[2] + primitive[3] * primitive[3])
    cons_list = [density, density * primitive[1], density * primitive[2], density * primitive[3], energy]
    flux_list = [element * normal_speed for element in cons_list]
    flux_list[1 + normal] = flux_list[1 + normal] + pressure
    flux_list[4] = flux_list[4] + pressure * normal_speed
    sound_speed = jnp.sqrt(GAMMA * pressure / density)
    return (jnp.stack(cons_list), jnp.stack(flux_list), normal_speed, sound_speed)

def hll_flux(lower_state, upper_state, normal):
    cons_low, flux_low, speed_low, sound_low = state_terms(lower_state, normal)
    cons_up, flux_up, speed_up, sound_up = state_terms(upper_state, normal)
    slowest = jnp.minimum(jnp.minimum(speed_low - sound_low, speed_up - sound_up), 0.0)
    fastest = jnp.maximum(jnp.maximum(speed_low + sound_low, speed_up + sound_up), 0.0)
    return (fastest * flux_low - slowest * flux_up + slowest * fastest * (cons_up - cons_low)) / (fastest - slowest)

def face_fluxes(primitive, lower_ghost, upper_ghost, dim_index, normal):
    length = primitive.shape[dim_index]

    def part_of(array, start, stop):
        return lax.slice_in_dim(array, start, stop, axis=dim_index)
    before = jnp.concatenate([part_of(lower_ghost, 1, 2), part_of(primitive, 0, length - 1)], axis=dim_index)
    before_two = jnp.concatenate([lower_ghost, part_of(primitive, 0, length - 2)], axis=dim_index)
    after = jnp.concatenate([part_of(primitive, 1, length), part_of(upper_ghost, 0, 1)], axis=dim_index)
    slopes = minmod(primitive - before, after - primitive)
    slopes_before = minmod(before - before_two, primitive - before)
    lower_faces = hll_flux(before + 0.5 * slopes_before, primitive - 0.5 * slopes, normal)
    last_cell = part_of(primitive, length - 1, length)
    ghost_near = part_of(upper_ghost, 0, 1)
    ghost_far = part_of(upper_ghost, 1, 2)
    ghost_slope = minmod(ghost_near - last_cell, ghost_far - ghost_near)
    end_face = hll_flux(last_cell + 0.5 * part_of(slopes, length - 1, length), ghost_near - 0.5 * ghost_slope, normal)
    upper_faces = jnp.concatenate([part_of(lower_faces, 1, length), end_face], axis=dim_index)
    return (upper_faces - lower_faces, lower_faces, end_face)

def advance(primitive, x_low, x_high, y_low, y_high, z_low, z_high):
    change = face_fluxes(primitive, x_low, x_high, 3, 0)[0] + face_fluxes(primitive, y_low, y_high, 1, 1)[0]
    z_change, z_lower, z_end = face_fluxes(primitive, z_low, z_high, 2, 2)
    return (change + z_change, z_lower[:, :, 0, :], z_end[:, :, 0, :])

def extract(box_cells, face_side):
    shaped = box_cells.reshape(box_cells.shape[:-1] + (CB, CB, CB))
    low_cut = shaped[..., CB - 4:CB - 1, 1:CB - 1, 1:CB - 1]
    high_cut = shaped[..., 1:4, 1:CB - 1, 1:CB - 1]
    return jnp.where((face_side == 1)[..., None, None, None, None], high_cut, low_cut)

def spread(values):
    return values[..., None, :, None, :, None]

def interpolate(coarse_cut, face_side):
    moved = jnp.moveaxis(coarse_cut, -4, 0)
    primitive = to_primitive(moved)
    centre = primitive[..., 1, 1:-1, 1:-1]
    slope_z = minmod(centre - primitive[..., 0, 1:-1, 1:-1], primitive[..., 2, 1:-1, 1:-1] - centre)
    slope_y = minmod(centre - primitive[..., 1, :-2, 1:-1], primitive[..., 1, 2:, 1:-1] - centre)
    slope_x = minmod(centre - primitive[..., 1, 1:-1, :-2], primitive[..., 1, 1:-1, 2:] - centre)
    offsets = (jnp.arange(RATIO, dtype=jnp.float32) + 0.5) / RATIO - 0.5
    z_offsets = jnp.where((face_side == 1)[..., None], offsets[:2], offsets[RATIO - 2:])
    fine = spread(centre) + spread(slope_z) * z_offsets[..., :, None, None, None, None]
    fine = fine + spread(slope_y) * offsets[:, None, None]
    fine = fine + spread(slope_x) * offsets
    fine = fine.reshape(fine.shape[:-5] + (2, QS, QS))
    return jnp.moveaxis(fine, 0, -4)

def assemble(pieces, face_index):
    chosen = pieces[:, :, face_index]
    return chosen.transpose(4, 0, 3, 6, 5, 1, 2, 7).reshape(5, PATCH_Y * PS, 2, PATCH_X * PS)

def coarsen(flux):
    across = PS // QS
    grouped = flux.reshape(5, PATCH_Y, across, CF, RATIO, PATCH_X, across, CF, RATIO)
    summed = grouped.sum(axis=(4, 8)) * (1.0 / RATIO)
    return summed.transpose(1, 4, 5, 2, 0, 3, 6)

def reference(fine_state, coarse_boxes, piece_owner, piece_box):
    across = PS // QS
    x_cells = PATCH_X * PS
    y_cells = PATCH_Y * PS
    conserved_all = fine_state.reshape(5, NYF, NXF, PS).transpose(0, 1, 3, 2)
    primitive_all = to_primitive(conserved_all)
    piece_ids = jnp.arange(PIECES, dtype=jnp.int32)
    device_ids = piece_ids // PIECE_DEV
    face_side = piece_ids % PIECE_DEV // (across * across) % 2
    box_index = (device_ids // N_DEV * N_DEV + piece_owner[:, 0]) * BOX_DEV + piece_box
    ghost_cells = interpolate(extract(coarse_boxes[box_index], face_side), face_side)
    ghost_by_device = ghost_cells.reshape(DEVICES, PATCH_Y, PATCH_X, 2, across, across, 5, 2, QS, QS)
    zero_index = jnp.zeros((), jnp.int32)

    def one_device(device):
        group_index = device // N_DEV
        dev_index = device % N_DEV
        y_start = (group_index * y_cells).astype(jnp.int32)
        x_start = (dev_index * x_cells).astype(jnp.int32)
        block = lax.dynamic_slice(primitive_all, (zero_index, y_start, zero_index, x_start), (5, y_cells, PS, x_cells))
        conserved_block = lax.dynamic_slice(conserved_all, (zero_index, y_start, zero_index, x_start), (5, y_cells, PS, x_cells))
        left_start = jnp.maximum(x_start - 2, 0).astype(jnp.int32)
        right_start = jnp.minimum(x_start + x_cells, NXF - 2).astype(jnp.int32)
        left_got = lax.dynamic_slice(primitive_all, (zero_index, y_start, zero_index, left_start), (5, y_cells, PS, 2))
        right_got = lax.dynamic_slice(primitive_all, (zero_index, y_start, zero_index, right_start), (5, y_cells, PS, 2))
        first_cell = block[..., :1]
        last_cell = block[..., x_cells - 1:]
        x_low = jnp.where(dev_index == 0, jnp.concatenate([first_cell, first_cell], axis=3), left_got)
        x_high = jnp.where(dev_index == N_DEV - 1, jnp.concatenate([last_cell, last_cell], axis=3), right_got)
        rows_low = ((y_start - 2 + jnp.arange(2, dtype=jnp.int32)) % NYF).astype(jnp.int32)
        rows_high = ((y_start + y_cells + jnp.arange(2, dtype=jnp.int32)) % NYF).astype(jnp.int32)
        y_low = lax.dynamic_slice_in_dim(jnp.take(primitive_all, rows_low, axis=1), x_start, x_cells, axis=3)
        y_high = lax.dynamic_slice_in_dim(jnp.take(primitive_all, rows_high, axis=1), x_start, x_cells, axis=3)
        pieces = ghost_by_device[device]
        z_low = assemble(pieces, 0)
        z_high = assemble(pieces, 1)
        change, bottom_flux, top_flux = advance(block, x_low, x_high, y_low, y_high, z_low, z_high)
        updated = conserved_block - DT_DX * change
        terms = jnp.stack([coarsen(bottom_flux), coarsen(top_flux)], axis=2).reshape(PIECE_DEV, 5 * CF * CF)
        return (updated, terms)
    updated, terms = lax.map(one_device, jnp.arange(DEVICES, dtype=jnp.int32))
    fine_next = updated.reshape(N_GROUP, N_DEV, 5, y_cells, PS, x_cells).transpose(2, 0, 3, 1, 5, 4).reshape(5, NYF, NXF * PS)
    segment_ids = face_side * NBOX + box_index
    summed = jax.ops.segment_sum(terms.reshape(PIECES, 5 * CF * CF), segment_ids, num_segments=2 * NBOX)
    flux_register = summed.reshape(2, NBOX, 5, CF * CF).transpose(2, 0, 3, 1).reshape(5, 2 * CF * CF, NBOX)
    return (fine_next, flux_register)
```

```python
import functools

import jax
import jax.numpy as jnp
from jax import lax
from jax.experimental import pallas as pl
from jax.experimental.pallas import tpu as pltpu
from jax.sharding import PartitionSpec as P

BOX_DEV = 128
PIECES_DEV = 32
MOST = 4
GAMMA = 1.4
DT_DX = 0.08
TILES = 16
ROWS = 32
LANES = 128
MESH = pl.DeviceIdType.MESH
F32 = jnp.float32
BF16 = jnp.bfloat16


def iota(shape, axis):
    return lax.broadcasted_iota(jnp.int32, shape, axis)


def minmod(a, b):
    return jnp.maximum(jnp.minimum(a, b), jnp.minimum(jnp.maximum(a, b), 0.0))


def primitives(q):
    r = 1.0 / q[0]
    u, v, w = q[1] * r, q[2] * r, q[3] * r
    p = (GAMMA - 1.0) * (q[4] - 0.5 * (q[1] * u + q[2] * v + q[3] * w))
    return [q[0], u, v, w, p]


def hll(low, up, normal):
    n = 1 + normal
    t1, t2 = [i for i in (1, 2, 3) if i != n]
    rl, ul, pl_ = low[0], low[n], low[4]
    ru, uu, pu = up[0], up[n], up[4]
    ql, qu = GAMMA * pl_, GAMMA * pu
    cl = ql * lax.rsqrt(ql * rl)
    cu = qu * lax.rsqrt(qu * ru)
    slow = jnp.minimum(jnp.minimum(ul - cl, uu - cu), 0.0)
    fast = jnp.maximum(jnp.maximum(ul + cl, uu + cu), 0.0)
    inverse = 1.0 / (fast - slow)
    a = fast * inverse
    b = slow * inverse
    e = slow * a
    aul = a * ul
    buu = b * uu
    wl = aul - e
    wu = e - buu
    ml = rl * wl
    mu = ru * wu
    nl, nu = ml * ul, mu * uu
    v1l, v1u = ml * low[t1], mu * up[t1]
    v2l, v2u = ml * low[t2], mu * up[t2]
    kinetic = (nl * ul + v1l * low[t1] + v2l * low[t2]) + (nu * uu + v1u * up[t1] + v2u * up[t2])
    flux = [None] * 5
    flux[0] = ml + mu
    flux[n] = (nl + nu) + (a * pl_ - b * pu)
    flux[t1] = v1l + v1u
    flux[t2] = v2l + v2u
    flux[4] = 0.5 * kinetic + (pl_ * (2.5 * wl + aul) + pu * (2.5 * wu - buu))
    return flux


def face(before_two, before, here, after, normal):
    low, up = [], []
    for f in range(5):
        d1 = here[f] - before[f]
        low.append(before[f] + 0.5 * minmod(before[f] - before_two[f], d1))
        up.append(here[f] - 0.5 * minmod(d1, after[f] - here[f]))
    return hll(low, up, normal)


def swap_tiles(tiles):
    tiles = list(tiles)
    lane = iota(tiles[0].shape, 1)
    for bit in range(4):
        step = 1 << bit
        odd = (lane & step) != 0
        for t in range(16):
            if t & step:
                continue
            a, b = tiles[t], tiles[t + step]
            tiles[t] = jnp.where(odd, pltpu.roll(b, step, 1), a)
            tiles[t + step] = jnp.where(odd, b, pltpu.roll(a, LANES - step, 1))
    return tiles


def parts(x):
    first = x.astype(BF16)
    rest = x - first.astype(F32)
    second = rest.astype(BF16)
    third = (rest - second.astype(F32)).astype(BF16)
    return first, second, third


def kernel(
    members, groups,
    fine, boxes, owner_in, box_in,
    out, register,
    q_s, w_s, p_s, fx_s, fy_s, ft_s, fz_s, o_s, cb_s, u_s, ids_s,
    ask_s, asked_s, give_s, got_s, sum_s, sums_s, ex_s, se_s, xh_s, yh_s, reg_s,
    load_sem, out_sem, ask_send, ask_recv, give_send, give_recv, sum_send, sum_recv, halo_send, halo_recv,
):
    me = lax.axis_index("dev")
    group = lax.axis_index("group")

    load_ids = [
        pltpu.make_async_copy(owner_in, ids_s.at[0:1], load_sem.at[0]),
        pltpu.make_async_copy(box_in, ids_s.at[1:2], load_sem.at[1]),
    ]
    load_boxes = pltpu.make_async_copy(boxes, cb_s, load_sem.at[2])
    load_fine = pltpu.make_async_copy(fine, q_s, load_sem.at[3])
    for copy in load_ids:
        copy.start()
    load_boxes.start()
    load_fine.start()

    barrier = pltpu.get_barrier_semaphore()
    north, south = lax.rem(group + 1, groups), lax.rem(group + groups - 1, groups)

    def greet(k, c):
        pl.semaphore_signal(
            barrier, inc=1, device_id=(group, lax.rem(me + k, members)), device_id_type=MESH
        )
        return c

    for y in (north, south):
        pl.semaphore_signal(barrier, inc=1, device_id=(y, me), device_id_type=MESH)
    lax.fori_loop(1, members, greet, 0)

    lane1 = iota((1, LANES), 1)
    row128 = iota((LANES, LANES), 0)
    lane128 = iota((LANES, LANES), 1)
    lane8 = iota((8, LANES), 1)
    row8 = iota((8, LANES), 0)

    for copy in load_ids:
        copy.wait()
    live = lane1 < PIECES_DEV
    owner = jnp.where(live, ids_s[0:1, :], -1)
    box = ids_s[1:2, :]
    row32, lane32 = iota((PIECES_DEV, LANES), 0), iota((PIECES_DEV, LANES), 1)
    owner_f = owner.astype(F32)
    owner_all = jnp.broadcast_to(owner_f, (PIECES_DEV, LANES))
    owner_col = jnp.sum(jnp.where(lane32 == row32, owner_all, 0.0), axis=1, keepdims=True)
    same = (jnp.broadcast_to(owner_col, (PIECES_DEV, LANES)) == owner_all) & (row32 < lane32)
    rank = jnp.sum(jnp.where(same, 1.0, 0.0), axis=0, keepdims=True)
    away = owner - me
    away = jnp.where(away < 0, away + members, away)
    slot = jnp.where(live, MOST * away + rank.astype(jnp.int32), -1)
    value = (box + 1 + BOX_DEV * (lane1 & 1)).astype(F32)
    hit = row128 == jnp.broadcast_to(slot, (LANES, LANES))
    asked_value = jnp.sum(
        jnp.where(hit, jnp.broadcast_to(value, (LANES, LANES)), 0.0), axis=1, keepdims=True
    )
    ask_s[...] = jnp.broadcast_to(asked_value, (LANES, LANES))

    pl.semaphore_wait(barrier, members + 1)

    def exchange(buffer, landed, send, recv, sign, part):
        def copy(k):
            return pltpu.make_async_remote_copy(
                src_ref=part(buffer, k),
                dst_ref=part(landed, k),
                send_sem=send,
                recv_sem=recv,
                device_id=(group, lax.rem(me + sign * k + members, members)),
                device_id_type=MESH,
            )

        def start(k, c):
            copy(k).start()
            return c

        lax.fori_loop(1, members, start, 0)

    def all_of(landed, send, recv, part):
        whole = part(landed)
        return pltpu.make_async_remote_copy(
            src_ref=whole, dst_ref=whole, send_sem=send, recv_sem=recv,
            device_id=(group, lax.rem(me + 1, members)), device_id_type=MESH,
        )

    one = lambda ref, k: ref.at[pl.ds(k * MOST, MOST)]
    one3 = lambda ref, k: ref.at[:, pl.ds(k * MOST, MOST)]
    rest = lambda ref: ref.at[pl.ds(MOST, (members - 1) * MOST)]
    rest3 = lambda ref: ref.at[:, pl.ds(MOST, (members - 1) * MOST)]

    exchange(ask_s, asked_s, ask_send, ask_recv, 1, one)
    asked_s[0:MOST, :] = ask_s[0:MOST, :]

    right, left = lax.rem(me + 1, members), lax.rem(me + members - 1, members)
    last = fine.shape[2] - LANES
    halos = [
        (fine.at[:, :, pl.ds(last, LANES)], xh_s.at[0], (group, right)),
        (fine.at[:, :, pl.ds(0, LANES)], xh_s.at[1], (group, left)),
        (fine.at[:, pl.ds(ROWS - 2, 2)], yh_s.at[0], (north, me)),
        (fine.at[:, pl.ds(0, 2)], yh_s.at[1], (south, me)),
    ]
    halo_copies = [
        pltpu.make_async_remote_copy(
            src_ref=src, dst_ref=dst, send_sem=halo_send.at[i], recv_sem=halo_recv.at[i],
            device_id=target, device_id_type=MESH,
        )
        for i, (src, dst, target) in enumerate(halos)
    ]
    for copy in halo_copies:
        copy.start()

    spots = []
    for ky in range(2):
        v = slot if ky == 0 else pltpu.roll(slot, LANES - 16, 1)
        v = jnp.where(lane1 < 16, v, 0)
        for step in (16, 32, 64):
            v = v + pltpu.roll(v, step, 1)
        odd = (lane1 & 1) != 0
        spots.append(jnp.where(odd, pltpu.roll(v, 1, 1), v))
        spots.append(jnp.where(odd, v, pltpu.roll(v, LANES - 1, 1)))
    spot = jnp.concatenate(
        [
            jnp.where(row128 == jnp.broadcast_to(s, (LANES, LANES)), 1.0, 0.0).astype(BF16)
            for s in spots
        ],
        axis=1,
    )

    load_boxes.wait()

    def table(n, c):
        rows = pl.ds(pl.multiple_of(n * 16, 16), 16)
        lane = iota((16, LANES), 1)
        lo = lane < 64
        t = [[cb_s[f, rows, k * LANES : (k + 1) * LANES] for k in range(4)] for f in range(5)]
        mid = primitives([jnp.where(lo, t[f][1], t[f][2]) for f in range(5)])
        below = primitives([jnp.where(lo, t[f][2], t[f][0]) for f in range(5)])
        above = primitives([jnp.where(lo, t[f][3], t[f][1]) for f in range(5)])
        first_y, first_x = (lane & 32) == 0, (lane & 4) == 0
        packed = []
        for f in range(5):
            m = mid[f]
            sz = minmod(m - pltpu.roll(below[f], 64, 1), pltpu.roll(above[f], 64, 1) - m)
            sy = minmod(m - pltpu.roll(m, 8, 1), pltpu.roll(m, LANES - 8, 1) - m)
            sx = minmod(m - pltpu.roll(m, 1, 1), pltpu.roll(m, LANES - 1, 1) - m)
            packed.append(
                jnp.where(
                    first_y,
                    jnp.where(first_x, pltpu.roll(m, LANES - 18, 1), pltpu.roll(sz, LANES - 14, 1)),
                    jnp.where(first_x, pltpu.roll(sy, 14, 1), pltpu.roll(sx, 18, 1)),
                )
            )
        cx, h, coef, cy = lane >> 5, (lane >> 4) & 1, (lane >> 2) & 3, lane & 3
        source = h * 64 + (coef >> 1) * 32 + cy * 8 + (coef & 1) * 4 + cx
        for pair in range(3):
            a = packed[2 * pair]
            b = packed[2 * pair + 1] if pair < 2 else a
            for side, tile in (
                (0, jnp.where(lo, pltpu.roll(a, 64, 1), b)),
                (1, jnp.where(lo, a, pltpu.roll(b, 64, 1))),
            ):
                moved = jnp.take_along_axis(tile, source, axis=1)
                where = pl.ds(pl.multiple_of(side * BOX_DEV + n * 16, 16), 16)
                for i, x in enumerate(parts(moved)):
                    u_s[i, where, pair * LANES : (pair + 1) * LANES] = x
        return c

    lax.fori_loop(0, BOX_DEV // 16, table, 0)

    load_fine.wait()

    def to_primitive(t, c):
        lanes = pl.ds(pl.multiple_of(t * LANES, LANES), LANES)
        w = primitives([q_s[f, :, lanes] for f in range(5)])
        for f in range(5):
            w_s[f, t + 1, 8 : 8 + ROWS, :] = w[f]
        return c

    lax.fori_loop(0, TILES, to_primitive, 0)

    all_of(asked_s, ask_send, ask_recv, rest).wait()
    asked = asked_s[...]
    lane_f = lane128.astype(F32)
    chosen = jnp.concatenate(
        [
            jnp.where(asked == lane_f + (1.0 + BOX_DEV * side), 1.0, 0.0).astype(BF16)
            for side in range(2)
        ],
        axis=1,
    )

    def dot(a, b, da, db):
        return lax.dot_general(a, b, (((da,), (db,)), ((), ())), preferred_element_type=F32)

    give = sum(dot(chosen, u_s[i], 1, 0) for i in range(3))
    for pair in range(3):
        give_s[pair] = give[:, pair * LANES : (pair + 1) * LANES]
    exchange(give_s, got_s, give_send, give_recv, -1, one3)
    got_s[:, 0:MOST, :] = give_s[:, 0:MOST, :]

    def pack(n, c):
        f, rb = n // 4, n % 4
        rows = pl.ds(pl.multiple_of(8 + rb * 8, 8), 8)
        tiles = swap_tiles([w_s[f, 1 + t, rows, :] for t in range(TILES)])
        for z in range(16):
            p_s[f, 2 + z, pl.ds(pl.multiple_of(rb * 8, 8), 8), :] = tiles[z]
        return c

    lax.fori_loop(0, 20, pack, 0)

    def z_face(k, half):
        rows = slice(16 * half, 16 * half + 16)
        w = [[p_s[f, k + i, rows, :] for f in range(5)] for i in range(4)]
        flux = face(*w, 2)
        for f in range(5):
            fz_s[f, k, rows, :] = flux[f]

    def z_inner(k, c):
        z_face(k, 0)
        z_face(k, 1)
        return c

    lax.fori_loop(2, 15, z_inner, 0)

    for copy in halo_copies:
        copy.wait()
    lane_r = iota((ROWS, LANES), 1)
    x_low = primitives([xh_s[0, f] for f in range(5)])
    x_high = primitives([xh_s[1, f] for f in range(5)])
    is_first = jnp.full((ROWS, LANES), me, jnp.int32) == 0
    is_last = jnp.full((ROWS, LANES), me, jnp.int32) == members - 1
    inner = slice(8, 8 + ROWS)
    for f in range(5):
        begin, end = w_s[f, 1, inner, :], w_s[f, TILES, inner, :]
        low_edge = jnp.where(lane_r < 112, pltpu.roll(begin, 96, 1), pltpu.roll(begin, 112, 1))
        high_edge = jnp.where(lane_r < 16, pltpu.roll(end, 16, 1), pltpu.roll(end, 32, 1))
        w_s[f, 0, inner, :] = jnp.where(is_first, low_edge, x_low[f])
        w_s[f, TILES + 1, inner, :] = jnp.where(is_last, high_edge, x_high[f])

    def y_halo(t, c):
        lanes = pl.ds(pl.multiple_of(t * LANES, LANES), LANES)
        low = primitives([yh_s[0, f, :, lanes] for f in range(5)])
        high = primitives([yh_s[1, f, :, lanes] for f in range(5)])
        for f in range(5):
            w_s[f, t + 1, 6:8, :] = low[f]
            w_s[f, t + 1, 8 + ROWS : 10 + ROWS, :] = high[f]
        return c

    lax.fori_loop(0, TILES, y_halo, 0)

    lane_h = iota((16, LANES), 1)

    def x_faces(t, c):
        after_tile = jnp.minimum(t + 1, TILES + 1)
        for half in range(2):
            rows = slice(8 + 16 * half, 24 + 16 * half)
            w = [[], [], [], []]
            for f in range(5):
                left_tile, tile, right_tile = w_s[f, t - 1, rows, :], w_s[f, t, rows, :], w_s[f, after_tile, rows, :]
                w[0].append(pltpu.roll(jnp.where(lane_h >= 96, left_tile, tile), 32, 1))
                w[1].append(pltpu.roll(jnp.where(lane_h >= 112, left_tile, tile), 16, 1))
                w[2].append(tile)
                w[3].append(pltpu.roll(jnp.where(lane_h < 16, right_tile, tile), LANES - 16, 1))
            flux = face(*w, 0)
            for f in range(5):
                fx_s[f, t, 16 * half : 16 * half + 16, :] = flux[f]
        return c

    lax.fori_loop(1, TILES + 2, x_faces, 0)

    top = face(*[[w_s[f, 1 : 1 + TILES, 38 + i, :] for f in range(5)] for i in range(4)], 1)
    for f in range(5):
        ft_s[f] = top[f]

    def y_faces(t, c):
        lanes = pl.ds(pl.multiple_of(t * LANES, LANES), LANES)
        for half in range(2):
            first = 6 + 16 * half
            w = [[w_s[f, t + 1, first + i : first + i + 16, :] for f in range(5)] for i in range(4)]
            flux = face(*w, 1)
            for f in range(5):
                fy_s[f, 16 * half : 16 * half + 16, :] = flux[f]
        for f in range(5):
            fy_s[f, ROWS : ROWS + 1, :] = ft_s[f, pl.ds(t, 1), :]
        for f in range(5):
            low, high = fx_s[f, t + 1], fx_s[f, t + 2]
            dx = pltpu.roll(jnp.where(lane_r < 16, high, low), LANES - 16, 1) - low
            dy = fy_s[f, 1 : 1 + ROWS, :] - fy_s[f, 0:ROWS, :]
            o_s[f, :, lanes] = q_s[f, :, lanes] - DT_DX * (dx + dy)
        return c

    lax.fori_loop(0, TILES, y_faces, 0)

    all_of(got_s, give_send, give_recv, rest3).wait()
    for pair in range(3):
        got = parts(got_s[pair])
        ex_s[pair] = sum(dot(x, spot, 0, 0) for x in got)
    t8, i8 = lane8 & 15, lane8 >> 4
    cx8 = 2 * (t8 & 1) + (i8 >> 2)
    ix_offset = ((i8 & 3).astype(F32) + 0.5) * 0.25 - 0.5
    iy_offset = ((row8 & 3).astype(F32) + 0.5) * 0.25 - 0.5
    cx32 = 2 * (lane_r & 1) + (lane_r >> 6)
    for pair in range(3):
        for kys in range(4):
            lanes = slice(kys * LANES, (kys + 1) * LANES)
            x = [ex_s[pair, 32 * cx : 32 * cx + 32, lanes] for cx in range(4)]
            se_s[pair, kys] = jnp.where(
                cx32 < 2, jnp.where(cx32 == 0, x[0], x[1]), jnp.where(cx32 == 2, x[2], x[3])
            )
    for f in range(5):
        pair, h = f // 2, f % 2
        for ky in range(2):
            for s in range(2):
                kys = 2 * ky + s
                for hh in range(2):
                    def coefficient(q):
                        r = h * 16 + q * 4 + 2 * hh
                        return jnp.where(
                            row8 < 4,
                            jnp.broadcast_to(se_s[pair, kys, r : r + 1, :], (8, LANES)),
                            jnp.broadcast_to(se_s[pair, kys, r + 1 : r + 2, :], (8, LANES)),
                        )

                    centre, slope_z = coefficient(0), coefficient(1)
                    slope_y, slope_x = coefficient(2), coefficient(3)
                    rows = slice(ky * 16 + hh * 8, ky * 16 + hh * 8 + 8)
                    for layer in range(2):
                        oz = (0.125, 0.375)[layer] if s == 0 else (-0.375, -0.125)[layer]
                        plane = layer if s == 0 else 18 + layer
                        p_s[f, plane, rows, :] = (
                            (centre + slope_z * oz) + slope_y * iy_offset
                        ) + slope_x * ix_offset

    for k in (0, 16):
        z_face(k, 0)
        z_face(k, 1)

    row_f = iota((ROWS, LANES), 0)
    keep = jnp.where(cx32 == (row_f & 3), 0.25, 0.0)
    odd1, odd2 = (row_f & 1) != 0, (row_f & 2) != 0
    terms = [[[] for _ in range(2)] for _ in range(2)]
    for s in range(2):
        for f in range(5):
            x = fz_s[f, 16 * s]
            x = x + jnp.where(odd1, pltpu.roll(x, 1, 0), pltpu.roll(x, ROWS - 1, 0))
            x = x + jnp.where(odd2, pltpu.roll(x, 2, 0), pltpu.roll(x, ROWS - 2, 0))
            x = x * keep
            terms[0][s].append(x[0:16])
            terms[1][s].append(x[16:32])
    pad = jnp.zeros((48, LANES), F32)
    all_terms = jnp.concatenate(
        [jnp.concatenate(terms[ky][s] + [pad], axis=0) for ky in range(2) for s in range(2)], axis=1
    )
    sum_s[...] = sum(dot(spot, x, 1, 1) for x in parts(all_terms))
    exchange(sum_s, sums_s, sum_send, sum_recv, 1, one)
    sums_s[0:MOST, :] = sum_s[0:MOST, :]

    for k in (1, 15):
        z_face(k, 0)
        z_face(k, 1)

    def finish(n, c):
        f, rb = n // 4, n % 4
        rows = pl.ds(pl.multiple_of(rb * 8, 8), 8)
        z = [fz_s[f, k, rows, :] for k in range(17)]
        tiles = swap_tiles([z[k + 1] - z[k] for k in range(16)])
        for t in range(TILES):
            lanes = slice(t * LANES, (t + 1) * LANES)
            o_s[f, rows, lanes] = o_s[f, rows, lanes] - DT_DX * tiles[t]
        return c

    lax.fori_loop(0, 20, finish, 0)
    store = pltpu.make_async_copy(o_s, out, out_sem.at[0])
    store.start()

    all_of(sums_s, sum_send, sum_recv, rest).wait()
    total = sum(dot(x, chosen, 0, 0) for x in parts(sums_s[...]))
    for f in range(5):
        for s in range(2):
            reg_s[f, 16 * s : 16 * s + 16, :] = total[
                16 * f : 16 * f + 16, s * LANES : (s + 1) * LANES
            ]
    store_register = pltpu.make_async_copy(reg_s, register, out_sem.at[1])
    store_register.start()
    store.wait()
    store_register.wait()


def local(fine_state, coarse_boxes, piece_owner, piece_box):
    members, groups = lax.axis_size("dev"), lax.axis_size("group")
    boxes = coarse_boxes.transpose(1, 0, 2)
    owner = jnp.pad(piece_owner.reshape(1, PIECES_DEV), ((0, 0), (0, LANES - PIECES_DEV)))
    box = jnp.pad(piece_box.reshape(1, PIECES_DEV), ((0, 0), (0, LANES - PIECES_DEV)))
    vmem = lambda *shape, dtype=F32: pltpu.VMEM(shape, dtype)
    dma = pltpu.SemaphoreType.DMA
    return pl.pallas_call(
        functools.partial(kernel, members, groups),
        out_shape=(
            jax.ShapeDtypeStruct(fine_state.shape, F32),
            jax.ShapeDtypeStruct((5, 32, BOX_DEV), F32),
        ),
        in_specs=[pl.BlockSpec(memory_space=pl.ANY)] * 4,
        out_specs=[pl.BlockSpec(memory_space=pl.ANY)] * 2,
        scratch_shapes=[
            vmem(5, ROWS, TILES * LANES),
            vmem(5, TILES + 2, 48, LANES),
            vmem(5, 20, ROWS, LANES),
            vmem(5, TILES + 2, ROWS, LANES),
            vmem(5, 40, LANES),
            vmem(5, TILES, LANES),
            vmem(5, 17, ROWS, LANES),
            vmem(5, ROWS, TILES * LANES),
            vmem(5, BOX_DEV, 512),
            vmem(3, 2 * BOX_DEV, 3 * LANES, dtype=BF16),
            vmem(8, LANES, dtype=jnp.int32),
            vmem(LANES, LANES),
            vmem(LANES, LANES),
            vmem(3, LANES, LANES),
            vmem(3, LANES, LANES),
            vmem(LANES, LANES),
            vmem(LANES, LANES),
            vmem(3, LANES, 4 * LANES),
            vmem(3, 4, 32, LANES),
            vmem(2, 5, ROWS, LANES),
            vmem(2, 5, 2, TILES * LANES),
            vmem(5, 32, BOX_DEV),
            dma((4,)),
            dma((2,)),
            dma, dma, dma, dma, dma, dma,
            dma((4,)),
            dma((4,)),
        ],
        compiler_params=pltpu.CompilerParams(
            collective_id=0, has_side_effects=True, vmem_limit_bytes=40 * 1024 * 1024
        ),
    )(fine_state, boxes, owner, box)


def solution(mesh):
    in_specs = (
        P(None, "group", "dev"),
        P(("group", "dev"), None, None),
        P(("group", "dev"), None),
        P(("group", "dev")),
    )
    out_specs = (P(None, "group", "dev"), P(None, None, ("group", "dev")))
    return jax.shard_map(local, mesh=mesh, in_specs=in_specs, out_specs=out_specs, check_vma=False)
```

```python
import functools

import jax
import jax.numpy as jnp
from jax import lax
from jax.experimental import pallas as pl
from jax.experimental.pallas import tpu as pltpu
from jax.sharding import PartitionSpec as P

BOX_DEV = 128
PIECES_DEV = 32
MOST = 4
GAMMA = 1.4
DT_DX = 0.08
TILES = 16
ROWS = 32
LANES = 128
MESH = pl.DeviceIdType.MESH
F32 = jnp.float32
BF16 = jnp.bfloat16


def iota(shape, axis):
    return lax.broadcasted_iota(jnp.int32, shape, axis)


def minmod(a, b):
    return jnp.maximum(jnp.minimum(a, b), jnp.minimum(jnp.maximum(a, b), 0.0))


def primitives(q):
    r = 1.0 / q[0]
    u, v, w = q[1] * r, q[2] * r, q[3] * r
    p = (GAMMA - 1.0) * (q[4] - 0.5 * (q[1] * u + q[2] * v + q[3] * w))
    return [q[0], u, v, w, p]


def hll(low, up, normal):
    n = 1 + normal
    t1, t2 = [i for i in (1, 2, 3) if i != n]
    rl, ul, pl_ = low[0], low[n], low[4]
    ru, uu, pu = up[0], up[n], up[4]
    ql, qu = GAMMA * pl_, GAMMA * pu
    cl = ql * lax.rsqrt(ql * rl)
    cu = qu * lax.rsqrt(qu * ru)
    slow = jnp.minimum(jnp.minimum(ul - cl, uu - cu), 0.0)
    fast = jnp.maximum(jnp.maximum(ul + cl, uu + cu), 0.0)
    inverse = 1.0 / (fast - slow)
    a = fast * inverse
    b = slow * inverse
    e = slow * a
    aul = a * ul
    buu = b * uu
    wl = aul - e
    wu = e - buu
    ml = rl * wl
    mu = ru * wu
    nl, nu = ml * ul, mu * uu
    v1l, v1u = ml * low[t1], mu * up[t1]
    v2l, v2u = ml * low[t2], mu * up[t2]
    kinetic = (nl * ul + v1l * low[t1] + v2l * low[t2]) + (nu * uu + v1u * up[t1] + v2u * up[t2])
    flux = [None] * 5
    flux[0] = ml + mu
    flux[n] = (nl + nu) + (a * pl_ - b * pu)
    flux[t1] = v1l + v1u
    flux[t2] = v2l + v2u
    flux[4] = 0.5 * kinetic + (pl_ * (2.5 * wl + aul) + pu * (2.5 * wu - buu))
    return flux


def face(before_two, before, here, after, normal):
    low, up = [], []
    for f in range(5):
        d1 = here[f] - before[f]
        low.append(before[f] + 0.5 * minmod(before[f] - before_two[f], d1))
        up.append(here[f] - 0.5 * minmod(d1, after[f] - here[f]))
    return hll(low, up, normal)


def swap_tiles(tiles):
    tiles = list(tiles)
    lane = iota(tiles[0].shape, 1)
    for bit in range(4):
        step = 1 << bit
        odd = (lane & step) != 0
        for t in range(16):
            if t & step:
                continue
            a, b = tiles[t], tiles[t + step]
            tiles[t] = jnp.where(odd, pltpu.roll(b, step, 1), a)
            tiles[t + step] = jnp.where(odd, b, pltpu.roll(a, LANES - step, 1))
    return tiles


def parts(x):
    first = x.astype(BF16)
    rest = x - first.astype(F32)
    second = rest.astype(BF16)
    third = (rest - second.astype(F32)).astype(BF16)
    return first, second, third


def kernel(
    members, groups,
    fine, boxes, owner_in, box_in,
    out, register,
    q_s, w_s, p_s, fx_s, fy_s, ft_s, fz_s, cb_s, u_s, owner_s, box_s,
    ask_s, asked_s, give_s, got_s, sum_s, sums_s, ex_s, se_s, xh_s, yh_s,
    load_sem, ask_send, ask_recv, give_send, give_recv, sum_send, sum_recv, halo_send, halo_recv,
):
    me = lax.axis_index("dev")
    group = lax.axis_index("group")

    load_ids = [
        pltpu.make_async_copy(owner_in, owner_s, load_sem.at[0]),
        pltpu.make_async_copy(box_in, box_s, load_sem.at[1]),
    ]
    load_boxes = pltpu.make_async_copy(boxes, cb_s, load_sem.at[2])
    load_fine = pltpu.make_async_copy(fine, q_s, load_sem.at[3])
    for copy in load_ids:
        copy.start()
    load_boxes.start()
    load_fine.start()

    barrier = pltpu.get_barrier_semaphore()
    north, south = lax.rem(group + 1, groups), lax.rem(group + groups - 1, groups)

    def greet(k, c):
        pl.semaphore_signal(
            barrier, inc=1, device_id=(group, lax.rem(me + k, members)), device_id_type=MESH
        )
        return c

    for y in (north, south):
        pl.semaphore_signal(barrier, inc=1, device_id=(y, me), device_id_type=MESH)
    lax.fori_loop(1, members, greet, 0)

    lane1 = iota((1, LANES), 1)
    row128 = iota((LANES, LANES), 0)
    lane128 = iota((LANES, LANES), 1)
    lane8 = iota((8, LANES), 1)
    row8 = iota((8, LANES), 0)

    for copy in load_ids:
        copy.wait()
    live = lane1 < PIECES_DEV
    fill = jnp.full((1, LANES - PIECES_DEV), -1, jnp.int32)
    owner = jnp.concatenate([owner_s[...], fill], axis=1)
    box = jnp.concatenate([box_s[...], fill], axis=1)
    row32, lane32 = iota((PIECES_DEV, LANES), 0), iota((PIECES_DEV, LANES), 1)
    owner_f = owner.astype(F32)
    owner_all = jnp.broadcast_to(owner_f, (PIECES_DEV, LANES))
    owner_col = jnp.sum(jnp.where(lane32 == row32, owner_all, 0.0), axis=1, keepdims=True)
    same = (jnp.broadcast_to(owner_col, (PIECES_DEV, LANES)) == owner_all) & (row32 < lane32)
    rank = jnp.sum(jnp.where(same, 1.0, 0.0), axis=0, keepdims=True)
    away = owner - me
    away = jnp.where(away < 0, away + members, away)
    slot = jnp.where(live, MOST * away + rank.astype(jnp.int32), -1)
    value = (box + 1 + BOX_DEV * (lane1 & 1)).astype(F32)
    hit = row128 == jnp.broadcast_to(slot, (LANES, LANES))
    asked_value = jnp.sum(
        jnp.where(hit, jnp.broadcast_to(value, (LANES, LANES)), 0.0), axis=1, keepdims=True
    )
    ask_s[...] = jnp.broadcast_to(asked_value, (LANES, LANES))

    pl.semaphore_wait(barrier, members + 1)

    def exchange(buffer, landed, send, recv, sign, part):
        def copy(k):
            return pltpu.make_async_remote_copy(
                src_ref=part(buffer, k),
                dst_ref=part(landed, k),
                send_sem=send,
                recv_sem=recv,
                device_id=(group, lax.rem(me + sign * k + members, members)),
                device_id_type=MESH,
            )

        def start(k, c):
            copy(k).start()
            return c

        lax.fori_loop(1, members, start, 0)

    def all_of(landed, send, recv, part):
        whole = part(landed)
        return pltpu.make_async_remote_copy(
            src_ref=whole, dst_ref=whole, send_sem=send, recv_sem=recv,
            device_id=(group, lax.rem(me + 1, members)), device_id_type=MESH,
        )

    one = lambda ref, k: ref.at[pl.ds(k * MOST, MOST)]
    one3 = lambda ref, k: ref.at[:, pl.ds(k * MOST, MOST)]
    rest = lambda ref: ref.at[pl.ds(MOST, (members - 1) * MOST)]
    rest3 = lambda ref: ref.at[:, pl.ds(MOST, (members - 1) * MOST)]

    exchange(ask_s, asked_s, ask_send, ask_recv, 1, one)
    asked_s[0:MOST, :] = ask_s[0:MOST, :]

    right, left = lax.rem(me + 1, members), lax.rem(me + members - 1, members)
    last = fine.shape[2] - LANES
    halos = [
        (fine.at[:, :, pl.ds(last, LANES)], xh_s.at[0], (group, right)),
        (fine.at[:, :, pl.ds(0, LANES)], xh_s.at[1], (group, left)),
        (fine.at[:, pl.ds(ROWS - 2, 2)], yh_s.at[0], (north, me)),
        (fine.at[:, pl.ds(0, 2)], yh_s.at[1], (south, me)),
    ]
    halo_copies = [
        pltpu.make_async_remote_copy(
            src_ref=src, dst_ref=dst, send_sem=halo_send.at[i], recv_sem=halo_recv.at[i],
            device_id=target, device_id_type=MESH,
        )
        for i, (src, dst, target) in enumerate(halos)
    ]
    for copy in halo_copies:
        copy.start()

    spots = []
    for ky in range(2):
        v = slot if ky == 0 else pltpu.roll(slot, LANES - 16, 1)
        v = jnp.where(lane1 < 16, v, 0)
        for step in (16, 32, 64):
            v = v + pltpu.roll(v, step, 1)
        odd = (lane1 & 1) != 0
        spots.append(jnp.where(odd, pltpu.roll(v, 1, 1), v))
        spots.append(jnp.where(odd, v, pltpu.roll(v, LANES - 1, 1)))
    spot = jnp.concatenate(
        [
            jnp.where(row128 == jnp.broadcast_to(s, (LANES, LANES)), 1.0, 0.0).astype(BF16)
            for s in spots
        ],
        axis=1,
    )

    load_boxes.wait()

    def table(n, c):
        rows = pl.ds(pl.multiple_of(n * 16, 16), 16)
        lane = iota((16, LANES), 1)
        lo = lane < 64
        t = [[cb_s[f, rows, k * LANES : (k + 1) * LANES] for k in range(4)] for f in range(5)]
        mid = primitives([jnp.where(lo, t[f][1], t[f][2]) for f in range(5)])
        below = primitives([jnp.where(lo, t[f][2], t[f][0]) for f in range(5)])
        above = primitives([jnp.where(lo, t[f][3], t[f][1]) for f in range(5)])
        first_y, first_x = (lane & 32) == 0, (lane & 4) == 0
        packed = []
        for f in range(5):
            m = mid[f]
            sz = minmod(m - pltpu.roll(below[f], 64, 1), pltpu.roll(above[f], 64, 1) - m)
            sy = minmod(m - pltpu.roll(m, 8, 1), pltpu.roll(m, LANES - 8, 1) - m)
            sx = minmod(m - pltpu.roll(m, 1, 1), pltpu.roll(m, LANES - 1, 1) - m)
            packed.append(
                jnp.where(
                    first_y,
                    jnp.where(first_x, pltpu.roll(m, LANES - 18, 1), pltpu.roll(sz, LANES - 14, 1)),
                    jnp.where(first_x, pltpu.roll(sy, 14, 1), pltpu.roll(sx, 18, 1)),
                )
            )
        cx, h, coef, cy = lane >> 5, (lane >> 4) & 1, (lane >> 2) & 3, lane & 3
        source = h * 64 + (coef >> 1) * 32 + cy * 8 + (coef & 1) * 4 + cx
        for pair in range(3):
            a = packed[2 * pair]
            b = packed[2 * pair + 1] if pair < 2 else a
            for side, tile in (
                (0, jnp.where(lo, pltpu.roll(a, 64, 1), b)),
                (1, jnp.where(lo, a, pltpu.roll(b, 64, 1))),
            ):
                moved = jnp.take_along_axis(tile, source, axis=1)
                where = pl.ds(pl.multiple_of(side * BOX_DEV + n * 16, 16), 16)
                for i, x in enumerate(parts(moved)):
                    u_s[i, where, pair * LANES : (pair + 1) * LANES] = x
        return c

    lax.fori_loop(0, BOX_DEV // 16, table, 0, unroll=4)

    load_fine.wait()

    def to_primitive(t, c):
        lanes = pl.ds(pl.multiple_of(t * LANES, LANES), LANES)
        w = primitives([q_s[f, :, lanes] for f in range(5)])
        for f in range(5):
            w_s[f, t + 1, 8 : 8 + ROWS, :] = w[f]
        return c

    lax.fori_loop(0, TILES, to_primitive, 0)

    all_of(asked_s, ask_send, ask_recv, rest).wait()
    asked = asked_s[...]
    lane_f = lane128.astype(F32)
    chosen = jnp.concatenate(
        [
            jnp.where(asked == lane_f + (1.0 + BOX_DEV * side), 1.0, 0.0).astype(BF16)
            for side in range(2)
        ],
        axis=1,
    )

    def dot(a, b, da, db):
        return lax.dot_general(a, b, (((da,), (db,)), ((), ())), preferred_element_type=F32)

    give = sum(dot(chosen, u_s[i], 1, 0) for i in range(3))
    for pair in range(3):
        give_s[pair] = give[:, pair * LANES : (pair + 1) * LANES]
    exchange(give_s, got_s, give_send, give_recv, -1, one3)
    got_s[:, 0:MOST, :] = give_s[:, 0:MOST, :]

    def pack(n, c):
        f, rb = n // 4, n % 4
        rows = pl.ds(pl.multiple_of(8 + rb * 8, 8), 8)
        tiles = swap_tiles([w_s[f, 1 + t, rows, :] for t in range(TILES)])
        for z in range(16):
            p_s[f, 2 + z, pl.ds(pl.multiple_of(rb * 8, 8), 8), :] = tiles[z]
        return c

    lax.fori_loop(0, 20, pack, 0, unroll=4)

    def z_face(k, half):
        rows = slice(16 * half, 16 * half + 16)
        w = [[p_s[f, k + i, rows, :] for f in range(5)] for i in range(4)]
        flux = face(*w, 2)
        for f in range(5):
            fz_s[f, k, rows, :] = flux[f]

    def z_inner(k, c):
        z_face(k, 0)
        z_face(k, 1)
        return c

    lax.fori_loop(2, 15, z_inner, 0)

    for copy in halo_copies:
        copy.wait()
    lane_r = iota((ROWS, LANES), 1)
    x_low = primitives([xh_s[0, f] for f in range(5)])
    x_high = primitives([xh_s[1, f] for f in range(5)])
    is_first = jnp.full((ROWS, LANES), me, jnp.int32) == 0
    is_last = jnp.full((ROWS, LANES), me, jnp.int32) == members - 1
    inner = slice(8, 8 + ROWS)
    for f in range(5):
        begin, end = w_s[f, 1, inner, :], w_s[f, TILES, inner, :]
        low_edge = jnp.where(lane_r < 112, pltpu.roll(begin, 96, 1), pltpu.roll(begin, 112, 1))
        high_edge = jnp.where(lane_r < 16, pltpu.roll(end, 16, 1), pltpu.roll(end, 32, 1))
        w_s[f, 0, inner, :] = jnp.where(is_first, low_edge, x_low[f])
        w_s[f, TILES + 1, inner, :] = jnp.where(is_last, high_edge, x_high[f])

    def y_halo(t, c):
        lanes = pl.ds(pl.multiple_of(t * LANES, LANES), LANES)
        low = primitives([yh_s[0, f, :, lanes] for f in range(5)])
        high = primitives([yh_s[1, f, :, lanes] for f in range(5)])
        for f in range(5):
            w_s[f, t + 1, 6:8, :] = low[f]
            w_s[f, t + 1, 8 + ROWS : 10 + ROWS, :] = high[f]
        return c

    lax.fori_loop(0, TILES, y_halo, 0)

    lane_h = iota((16, LANES), 1)

    def x_faces(t, c):
        after_tile = jnp.minimum(t + 1, TILES + 1)
        for half in range(2):
            rows = slice(8 + 16 * half, 24 + 16 * half)
            w = [[], [], [], []]
            for f in range(5):
                left_tile, tile, right_tile = w_s[f, t - 1, rows, :], w_s[f, t, rows, :], w_s[f, after_tile, rows, :]
                w[0].append(pltpu.roll(jnp.where(lane_h >= 96, left_tile, tile), 32, 1))
                w[1].append(pltpu.roll(jnp.where(lane_h >= 112, left_tile, tile), 16, 1))
                w[2].append(tile)
                w[3].append(pltpu.roll(jnp.where(lane_h < 16, right_tile, tile), LANES - 16, 1))
            flux = face(*w, 0)
            for f in range(5):
                fx_s[f, t, 16 * half : 16 * half + 16, :] = flux[f]
        return c

    lax.fori_loop(1, TILES + 2, x_faces, 0)

    top = face(*[[w_s[f, 1 : 1 + TILES, 38 + i, :] for f in range(5)] for i in range(4)], 1)
    for f in range(5):
        ft_s[f] = top[f]

    def y_faces(t, c):
        lanes = pl.ds(pl.multiple_of(t * LANES, LANES), LANES)
        for half in range(2):
            first = 6 + 16 * half
            w = [[w_s[f, t + 1, first + i : first + i + 16, :] for f in range(5)] for i in range(4)]
            flux = face(*w, 1)
            for f in range(5):
                fy_s[f, 16 * half : 16 * half + 16, :] = flux[f]
        for f in range(5):
            fy_s[f, ROWS : ROWS + 1, :] = ft_s[f, pl.ds(t, 1), :]
        for f in range(5):
            low, high = fx_s[f, t + 1], fx_s[f, t + 2]
            dx = pltpu.roll(jnp.where(lane_r < 16, high, low), LANES - 16, 1) - low
            dy = fy_s[f, 1 : 1 + ROWS, :] - fy_s[f, 0:ROWS, :]
            out[f, :, lanes] = q_s[f, :, lanes] - DT_DX * (dx + dy)
        return c

    lax.fori_loop(0, TILES, y_faces, 0)

    all_of(got_s, give_send, give_recv, rest3).wait()
    for pair in range(3):
        got = parts(got_s[pair])
        ex_s[pair] = sum(dot(x, spot, 0, 0) for x in got)
    t8, i8 = lane8 & 15, lane8 >> 4
    cx8 = 2 * (t8 & 1) + (i8 >> 2)
    ix_offset = ((i8 & 3).astype(F32) + 0.5) * 0.25 - 0.5
    iy_offset = ((row8 & 3).astype(F32) + 0.5) * 0.25 - 0.5
    cx32 = 2 * (lane_r & 1) + (lane_r >> 6)
    for pair in range(3):
        for kys in range(4):
            lanes = slice(kys * LANES, (kys + 1) * LANES)
            x = [ex_s[pair, 32 * cx : 32 * cx + 32, lanes] for cx in range(4)]
            se_s[pair, kys] = jnp.where(
                cx32 < 2, jnp.where(cx32 == 0, x[0], x[1]), jnp.where(cx32 == 2, x[2], x[3])
            )
    for f in range(5):
        pair, h = f // 2, f % 2
        for ky in range(2):
            for s in range(2):
                kys = 2 * ky + s
                for hh in range(2):
                    def coefficient(q):
                        r = h * 16 + q * 4 + 2 * hh
                        return jnp.where(
                            row8 < 4,
                            jnp.broadcast_to(se_s[pair, kys, r : r + 1, :], (8, LANES)),
                            jnp.broadcast_to(se_s[pair, kys, r + 1 : r + 2, :], (8, LANES)),
                        )

                    centre, slope_z = coefficient(0), coefficient(1)
                    slope_y, slope_x = coefficient(2), coefficient(3)
                    rows = slice(ky * 16 + hh * 8, ky * 16 + hh * 8 + 8)
                    for layer in range(2):
                        oz = (0.125, 0.375)[layer] if s == 0 else (-0.375, -0.125)[layer]
                        plane = layer if s == 0 else 18 + layer
                        p_s[f, plane, rows, :] = (
                            (centre + slope_z * oz) + slope_y * iy_offset
                        ) + slope_x * ix_offset

    for k in (0, 16):
        z_face(k, 0)
        z_face(k, 1)

    row_f = iota((ROWS, LANES), 0)
    keep = jnp.where(cx32 == (row_f & 3), 0.25, 0.0)
    odd1, odd2 = (row_f & 1) != 0, (row_f & 2) != 0
    terms = [[[] for _ in range(2)] for _ in range(2)]
    for s in range(2):
        for f in range(5):
            x = fz_s[f, 16 * s]
            x = x + jnp.where(odd1, pltpu.roll(x, 1, 0), pltpu.roll(x, ROWS - 1, 0))
            x = x + jnp.where(odd2, pltpu.roll(x, 2, 0), pltpu.roll(x, ROWS - 2, 0))
            x = x * keep
            terms[0][s].append(x[0:16])
            terms[1][s].append(x[16:32])
    pad = jnp.zeros((48, LANES), F32)
    all_terms = jnp.concatenate(
        [jnp.concatenate(terms[ky][s] + [pad], axis=0) for ky in range(2) for s in range(2)], axis=1
    )
    sum_s[...] = sum(dot(spot, x, 1, 1) for x in parts(all_terms))
    exchange(sum_s, sums_s, sum_send, sum_recv, 1, one)
    sums_s[0:MOST, :] = sum_s[0:MOST, :]

    for k in (1, 15):
        z_face(k, 0)
        z_face(k, 1)

    def finish(n, c):
        f, rb = n // 4, n % 4
        rows = pl.ds(pl.multiple_of(rb * 8, 8), 8)
        z = [fz_s[f, k, rows, :] for k in range(17)]
        tiles = swap_tiles([z[k + 1] - z[k] for k in range(16)])
        for t in range(TILES):
            lanes = slice(t * LANES, (t + 1) * LANES)
            out[f, rows, lanes] = out[f, rows, lanes] - DT_DX * tiles[t]
        return c

    lax.fori_loop(0, 20, finish, 0, unroll=4)

    all_of(sums_s, sum_send, sum_recv, rest).wait()
    total = sum(dot(x, chosen, 0, 0) for x in parts(sums_s[...]))
    for f in range(5):
        for s in range(2):
            register[f, 16 * s : 16 * s + 16, :] = total[
                16 * f : 16 * f + 16, s * LANES : (s + 1) * LANES
            ]


def local(fine_state, coarse_boxes, piece_owner, piece_box):
    members, groups = lax.axis_size("dev"), lax.axis_size("group")
    boxes = coarse_boxes.transpose(1, 0, 2)
    owner = piece_owner.reshape(1, PIECES_DEV)
    box = piece_box.reshape(1, PIECES_DEV)
    vmem = lambda *shape, dtype=F32: pltpu.VMEM(shape, dtype)
    dma = pltpu.SemaphoreType.DMA
    return pl.pallas_call(
        functools.partial(kernel, members, groups),
        out_shape=(
            vmem(*fine_state.shape),
            vmem(5, 32, BOX_DEV),
        ),
        in_specs=[pl.BlockSpec(memory_space=pltpu.HBM)] * 4,
        out_specs=[pl.BlockSpec(memory_space=pltpu.VMEM)] * 2,
        scratch_shapes=[
            vmem(5, ROWS, TILES * LANES),
            vmem(5, TILES + 2, 48, LANES),
            vmem(5, 20, ROWS, LANES),
            vmem(5, TILES + 2, ROWS, LANES),
            vmem(5, 40, LANES),
            vmem(5, TILES, LANES),
            vmem(5, 17, ROWS, LANES),
            vmem(5, BOX_DEV, 512),
            vmem(3, 2 * BOX_DEV, 3 * LANES, dtype=BF16),
            vmem(1, PIECES_DEV, dtype=jnp.int32),
            vmem(1, PIECES_DEV, dtype=jnp.int32),
            vmem(LANES, LANES),
            vmem(LANES, LANES),
            vmem(3, LANES, LANES),
            vmem(3, LANES, LANES),
            vmem(LANES, LANES),
            vmem(LANES, LANES),
            vmem(3, LANES, 4 * LANES),
            vmem(3, 4, 32, LANES),
            vmem(2, 5, ROWS, LANES),
            vmem(2, 5, 2, TILES * LANES),
            dma((4,)),
            dma, dma, dma, dma, dma, dma,
            dma((4,)),
            dma((4,)),
        ],
        compiler_params=pltpu.CompilerParams(
            collective_id=0, has_side_effects=True, vmem_limit_bytes=40 * 1024 * 1024
        ),
    )(*[pltpu.with_memory_space_constraint(x, pltpu.HBM) for x in (fine_state, boxes, owner, box)])


def solution(mesh):
    in_specs = (
        P(None, "group", "dev"),
        P(("group", "dev"), None, None),
        P(("group", "dev"), None),
        P(("group", "dev")),
    )
    out_specs = (P(None, "group", "dev"), P(None, None, ("group", "dev")))
    return jax.shard_map(local, mesh=mesh, in_specs=in_specs, out_specs=out_specs, check_vma=False)
```

```python
import functools

import jax
import jax.numpy as jnp
from jax import lax
from jax.experimental import pallas as pl
from jax.experimental.pallas import tpu as pltpu
from jax.sharding import PartitionSpec as P

BOX_DEV = 128
PIECES_DEV = 32
MOST = 4
GAMMA = 1.4
DT_DX = 0.08
TILES = 16
ROWS = 32
LANES = 128
MESH = pl.DeviceIdType.MESH
F32 = jnp.float32
BF16 = jnp.bfloat16


def iota(shape, axis):
    return lax.broadcasted_iota(jnp.int32, shape, axis)


def minmod(a, b):
    return jnp.maximum(jnp.minimum(a, b), jnp.minimum(jnp.maximum(a, b), 0.0))


def primitives(q):
    r = 1.0 / q[0]
    u, v, w = q[1] * r, q[2] * r, q[3] * r
    p = (GAMMA - 1.0) * (q[4] - 0.5 * (q[1] * u + q[2] * v + q[3] * w))
    return [q[0], u, v, w, p]


def hll(low, up, normal):
    n = 1 + normal
    t1, t2 = [i for i in (1, 2, 3) if i != n]
    rl, ul, pl_ = low[0], low[n], low[4]
    ru, uu, pu = up[0], up[n], up[4]
    ql, qu = GAMMA * pl_, GAMMA * pu
    cl = ql * lax.rsqrt(ql * rl)
    cu = qu * lax.rsqrt(qu * ru)
    slow = jnp.minimum(jnp.minimum(ul - cl, uu - cu), 0.0)
    fast = jnp.maximum(jnp.maximum(ul + cl, uu + cu), 0.0)
    inverse = 1.0 / (fast - slow)
    a = fast * inverse
    b = slow * inverse
    e = slow * a
    aul = a * ul
    buu = b * uu
    wl = aul - e
    wu = e - buu
    ml = rl * wl
    mu = ru * wu
    nl, nu = ml * ul, mu * uu
    v1l, v1u = ml * low[t1], mu * up[t1]
    v2l, v2u = ml * low[t2], mu * up[t2]
    kinetic = (nl * ul + v1l * low[t1] + v2l * low[t2]) + (nu * uu + v1u * up[t1] + v2u * up[t2])
    flux = [None] * 5
    flux[0] = ml + mu
    flux[n] = (nl + nu) + (a * pl_ - b * pu)
    flux[t1] = v1l + v1u
    flux[t2] = v2l + v2u
    flux[4] = 0.5 * kinetic + (pl_ * (2.5 * wl + aul) + pu * (2.5 * wu - buu))
    return flux


def face(before_two, before, here, after, normal):
    low, up = [], []
    for f in range(5):
        d1 = here[f] - before[f]
        low.append(before[f] + 0.5 * minmod(before[f] - before_two[f], d1))
        up.append(here[f] - 0.5 * minmod(d1, after[f] - here[f]))
    return hll(low, up, normal)


def swap_tiles(tiles):
    tiles = list(tiles)
    lane = iota(tiles[0].shape, 1)
    for bit in range(4):
        step = 1 << bit
        odd = (lane & step) != 0
        for t in range(16):
            if t & step:
                continue
            a, b = tiles[t], tiles[t + step]
            tiles[t] = jnp.where(odd, pltpu.roll(b, step, 1), a)
            tiles[t + step] = jnp.where(odd, b, pltpu.roll(a, LANES - step, 1))
    return tiles


def parts(x):
    first = x.astype(BF16)
    rest = x - first.astype(F32)
    second = rest.astype(BF16)
    third = (rest - second.astype(F32)).astype(BF16)
    return first, second, third


def kernel(
    members, groups,
    fine, boxes, owner_in, box_in,
    out, register,
    q_s, w_s, p_s, fx_s, fy_s, ft_s, fz_s, cb_s, u_s, owner_s, box_s,
    ask_s, asked_s, give_s, got_s, sum_s, sums_s, ex_s, se_s, xh_s, yh_s,
    load_sem, ask_send, ask_recv, give_send, give_recv, sum_send, sum_recv, halo_send, halo_recv,
):
    me = lax.axis_index("dev")
    group = lax.axis_index("group")

    load_ids = [
        pltpu.make_async_copy(owner_in, owner_s, load_sem.at[0]),
        pltpu.make_async_copy(box_in, box_s, load_sem.at[1]),
    ]
    load_boxes = pltpu.make_async_copy(boxes, cb_s, load_sem.at[2])
    load_fine = pltpu.make_async_copy(fine, q_s, load_sem.at[3])
    for copy in load_ids:
        copy.start()
    load_boxes.start()
    load_fine.start()

    barrier = pltpu.get_barrier_semaphore()
    north, south = lax.rem(group + 1, groups), lax.rem(group + groups - 1, groups)

    def greet(k, c):
        pl.semaphore_signal(
            barrier, inc=1, device_id=(group, lax.rem(me + k, members)), device_id_type=MESH
        )
        return c

    for y in (north, south):
        pl.semaphore_signal(barrier, inc=1, device_id=(y, me), device_id_type=MESH)
    lax.fori_loop(1, members, greet, 0)

    lane1 = iota((1, LANES), 1)
    row128 = iota((LANES, LANES), 0)
    lane128 = iota((LANES, LANES), 1)
    lane8 = iota((8, LANES), 1)
    row8 = iota((8, LANES), 0)

    for copy in load_ids:
        copy.wait()
    live = lane1 < PIECES_DEV
    fill = jnp.full((1, LANES - PIECES_DEV), -1, jnp.int32)
    owner = jnp.concatenate([owner_s[...], fill], axis=1)
    box = jnp.concatenate([box_s[...], fill], axis=1)
    row32, lane32 = iota((PIECES_DEV, LANES), 0), iota((PIECES_DEV, LANES), 1)
    owner_f = owner.astype(F32)
    owner_all = jnp.broadcast_to(owner_f, (PIECES_DEV, LANES))
    owner_col = jnp.sum(jnp.where(lane32 == row32, owner_all, 0.0), axis=1, keepdims=True)
    same = (jnp.broadcast_to(owner_col, (PIECES_DEV, LANES)) == owner_all) & (row32 < lane32)
    rank = jnp.sum(jnp.where(same, 1.0, 0.0), axis=0, keepdims=True)
    away = owner - me
    away = jnp.where(away < 0, away + members, away)
    slot = jnp.where(live, MOST * away + rank.astype(jnp.int32), -1)
    value = (box + 1 + BOX_DEV * (lane1 & 1)).astype(F32)
    hit = row128 == jnp.broadcast_to(slot, (LANES, LANES))
    asked_value = jnp.sum(
        jnp.where(hit, jnp.broadcast_to(value, (LANES, LANES)), 0.0), axis=1, keepdims=True
    )
    ask_s[...] = jnp.broadcast_to(asked_value, (LANES, LANES))

    pl.semaphore_wait(barrier, members + 1)

    def exchange(buffer, landed, send, recv, sign, part):
        def copy(k):
            return pltpu.make_async_remote_copy(
                src_ref=part(buffer, k),
                dst_ref=part(landed, k),
                send_sem=send,
                recv_sem=recv,
                device_id=(group, lax.rem(me + sign * k + members, members)),
                device_id_type=MESH,
            )

        def start(k, c):
            copy(k).start()
            return c

        lax.fori_loop(1, members, start, 0)

    def all_of(landed, send, recv, part):
        whole = part(landed)
        return pltpu.make_async_remote_copy(
            src_ref=whole, dst_ref=whole, send_sem=send, recv_sem=recv,
            device_id=(group, lax.rem(me + 1, members)), device_id_type=MESH,
        )

    one = lambda ref, k: ref.at[pl.ds(k * MOST, MOST)]
    one3 = lambda ref, k: ref.at[:, pl.ds(k * MOST, MOST)]
    rest = lambda ref: ref.at[pl.ds(MOST, (members - 1) * MOST)]
    rest3 = lambda ref: ref.at[:, pl.ds(MOST, (members - 1) * MOST)]

    exchange(ask_s, asked_s, ask_send, ask_recv, 1, one)
    asked_s[0:MOST, :] = ask_s[0:MOST, :]

    right, left = lax.rem(me + 1, members), lax.rem(me + members - 1, members)
    last = fine.shape[2] - LANES
    halos = [
        (fine.at[:, :, pl.ds(last, LANES)], xh_s.at[0], (group, right)),
        (fine.at[:, :, pl.ds(0, LANES)], xh_s.at[1], (group, left)),
        (fine.at[:, pl.ds(ROWS - 2, 2)], yh_s.at[0], (north, me)),
        (fine.at[:, pl.ds(0, 2)], yh_s.at[1], (south, me)),
    ]
    halo_copies = [
        pltpu.make_async_remote_copy(
            src_ref=src, dst_ref=dst, send_sem=halo_send.at[i], recv_sem=halo_recv.at[i],
            device_id=target, device_id_type=MESH,
        )
        for i, (src, dst, target) in enumerate(halos)
    ]
    for copy in halo_copies:
        copy.start()

    spots = []
    for ky in range(2):
        v = slot if ky == 0 else pltpu.roll(slot, LANES - 16, 1)
        v = jnp.where(lane1 < 16, v, 0)
        for step in (16, 32, 64):
            v = v + pltpu.roll(v, step, 1)
        odd = (lane1 & 1) != 0
        spots.append(jnp.where(odd, pltpu.roll(v, 1, 1), v))
        spots.append(jnp.where(odd, v, pltpu.roll(v, LANES - 1, 1)))
    spot = jnp.concatenate(
        [
            jnp.where(row128 == jnp.broadcast_to(s, (LANES, LANES)), 1.0, 0.0).astype(BF16)
            for s in spots
        ],
        axis=1,
    )

    load_boxes.wait()

    def table(n, c):
        rows = pl.ds(pl.multiple_of(n * 16, 16), 16)
        lane = iota((16, LANES), 1)
        lo = lane < 64
        t = [[cb_s[f, rows, k * LANES : (k + 1) * LANES] for k in range(4)] for f in range(5)]
        mid = primitives([jnp.where(lo, t[f][1], t[f][2]) for f in range(5)])
        below = primitives([jnp.where(lo, t[f][2], t[f][0]) for f in range(5)])
        above = primitives([jnp.where(lo, t[f][3], t[f][1]) for f in range(5)])
        first_y, first_x = (lane & 32) == 0, (lane & 4) == 0
        packed = []
        for f in range(5):
            m = mid[f]
            sz = minmod(m - pltpu.roll(below[f], 64, 1), pltpu.roll(above[f], 64, 1) - m)
            sy = minmod(m - pltpu.roll(m, 8, 1), pltpu.roll(m, LANES - 8, 1) - m)
            sx = minmod(m - pltpu.roll(m, 1, 1), pltpu.roll(m, LANES - 1, 1) - m)
            packed.append(
                jnp.where(
                    first_y,
                    jnp.where(first_x, pltpu.roll(m, LANES - 18, 1), pltpu.roll(sz, LANES - 14, 1)),
                    jnp.where(first_x, pltpu.roll(sy, 14, 1), pltpu.roll(sx, 18, 1)),
                )
            )
        cx, h, coef, cy = lane >> 5, (lane >> 4) & 1, (lane >> 2) & 3, lane & 3
        source = h * 64 + (coef >> 1) * 32 + cy * 8 + (coef & 1) * 4 + cx
        for pair in range(3):
            a = packed[2 * pair]
            b = packed[2 * pair + 1] if pair < 2 else a
            for side, tile in (
                (0, jnp.where(lo, pltpu.roll(a, 64, 1), b)),
                (1, jnp.where(lo, a, pltpu.roll(b, 64, 1))),
            ):
                moved = jnp.take_along_axis(tile, source, axis=1)
                where = pl.ds(pl.multiple_of(side * BOX_DEV + n * 16, 16), 16)
                for i, x in enumerate(parts(moved)):
                    u_s[i, where, pair * LANES : (pair + 1) * LANES] = x
        return c

    lax.fori_loop(0, BOX_DEV // 16, table, 0, unroll=4)

    load_fine.wait()

    def to_primitive(t, c):
        lanes = pl.ds(pl.multiple_of(t * LANES, LANES), LANES)
        w = primitives([q_s[f, :, lanes] for f in range(5)])
        for f in range(5):
            w_s[f, t + 1, 8 : 8 + ROWS, :] = w[f]
        return c

    lax.fori_loop(0, TILES, to_primitive, 0)

    def pack(n, c):
        f, rb = n // 4, n % 4
        rows = pl.ds(pl.multiple_of(8 + rb * 8, 8), 8)
        tiles = swap_tiles([w_s[f, 1 + t, rows, :] for t in range(TILES)])
        for z in range(16):
            p_s[f, 2 + z, pl.ds(pl.multiple_of(rb * 8, 8), 8), :] = tiles[z]
        return c

    lax.fori_loop(0, 20, pack, 0, unroll=4)

    all_of(asked_s, ask_send, ask_recv, rest).wait()
    asked = asked_s[...]
    lane_f = lane128.astype(F32)
    chosen = jnp.concatenate(
        [
            jnp.where(asked == lane_f + (1.0 + BOX_DEV * side), 1.0, 0.0).astype(BF16)
            for side in range(2)
        ],
        axis=1,
    )

    def dot(a, b, da, db):
        return lax.dot_general(a, b, (((da,), (db,)), ((), ())), preferred_element_type=F32)

    give = sum(dot(chosen, u_s[i], 1, 0) for i in range(3))
    for pair in range(3):
        give_s[pair] = give[:, pair * LANES : (pair + 1) * LANES]
    exchange(give_s, got_s, give_send, give_recv, -1, one3)
    got_s[:, 0:MOST, :] = give_s[:, 0:MOST, :]

    def z_face(k, half):
        rows = slice(16 * half, 16 * half + 16)
        w = [[p_s[f, k + i, rows, :] for f in range(5)] for i in range(4)]
        flux = face(*w, 2)
        for f in range(5):
            fz_s[f, k, rows, :] = flux[f]

    def z_inner(k, c):
        z_face(k, 0)
        z_face(k, 1)
        return c

    lax.fori_loop(2, 15, z_inner, 0)

    for copy in halo_copies:
        copy.wait()
    lane_r = iota((ROWS, LANES), 1)
    x_low = primitives([xh_s[0, f] for f in range(5)])
    x_high = primitives([xh_s[1, f] for f in range(5)])
    is_first = jnp.full((ROWS, LANES), me, jnp.int32) == 0
    is_last = jnp.full((ROWS, LANES), me, jnp.int32) == members - 1
    inner = slice(8, 8 + ROWS)
    for f in range(5):
        begin, end = w_s[f, 1, inner, :], w_s[f, TILES, inner, :]
        low_edge = jnp.where(lane_r < 112, pltpu.roll(begin, 96, 1), pltpu.roll(begin, 112, 1))
        high_edge = jnp.where(lane_r < 16, pltpu.roll(end, 16, 1), pltpu.roll(end, 32, 1))
        w_s[f, 0, inner, :] = jnp.where(is_first, low_edge, x_low[f])
        w_s[f, TILES + 1, inner, :] = jnp.where(is_last, high_edge, x_high[f])

    def y_halo(t, c):
        lanes = pl.ds(pl.multiple_of(t * LANES, LANES), LANES)
        low = primitives([yh_s[0, f, :, lanes] for f in range(5)])
        high = primitives([yh_s[1, f, :, lanes] for f in range(5)])
        for f in range(5):
            w_s[f, t + 1, 6:8, :] = low[f]
            w_s[f, t + 1, 8 + ROWS : 10 + ROWS, :] = high[f]
        return c

    lax.fori_loop(0, TILES, y_halo, 0)

    lane_h = iota((16, LANES), 1)

    def x_faces(t, c):
        after_tile = jnp.minimum(t + 1, TILES + 1)
        for half in range(2):
            rows = slice(8 + 16 * half, 24 + 16 * half)
            w = [[], [], [], []]
            for f in range(5):
                left_tile, tile, right_tile = w_s[f, t - 1, rows, :], w_s[f, t, rows, :], w_s[f, after_tile, rows, :]
                w[0].append(pltpu.roll(jnp.where(lane_h >= 96, left_tile, tile), 32, 1))
                w[1].append(pltpu.roll(jnp.where(lane_h >= 112, left_tile, tile), 16, 1))
                w[2].append(tile)
                w[3].append(pltpu.roll(jnp.where(lane_h < 16, right_tile, tile), LANES - 16, 1))
            flux = face(*w, 0)
            for f in range(5):
                fx_s[f, t, 16 * half : 16 * half + 16, :] = flux[f]
        return c

    lax.fori_loop(1, TILES + 2, x_faces, 0)

    all_of(got_s, give_send, give_recv, rest3).wait()
    for pair in range(3):
        got = parts(got_s[pair])
        ex_s[pair] = sum(dot(x, spot, 0, 0) for x in got)
    t8, i8 = lane8 & 15, lane8 >> 4
    cx8 = 2 * (t8 & 1) + (i8 >> 2)
    ix_offset = ((i8 & 3).astype(F32) + 0.5) * 0.25 - 0.5
    iy_offset = ((row8 & 3).astype(F32) + 0.5) * 0.25 - 0.5
    cx32 = 2 * (lane_r & 1) + (lane_r >> 6)
    for pair in range(3):
        for kys in range(4):
            lanes = slice(kys * LANES, (kys + 1) * LANES)
            x = [ex_s[pair, 32 * cx : 32 * cx + 32, lanes] for cx in range(4)]
            se_s[pair, kys] = jnp.where(
                cx32 < 2, jnp.where(cx32 == 0, x[0], x[1]), jnp.where(cx32 == 2, x[2], x[3])
            )
    for f in range(5):
        pair, h = f // 2, f % 2
        for ky in range(2):
            for s in range(2):
                kys = 2 * ky + s
                for hh in range(2):
                    def coefficient(q):
                        r = h * 16 + q * 4 + 2 * hh
                        return jnp.where(
                            row8 < 4,
                            jnp.broadcast_to(se_s[pair, kys, r : r + 1, :], (8, LANES)),
                            jnp.broadcast_to(se_s[pair, kys, r + 1 : r + 2, :], (8, LANES)),
                        )

                    centre, slope_z = coefficient(0), coefficient(1)
                    slope_y, slope_x = coefficient(2), coefficient(3)
                    rows = slice(ky * 16 + hh * 8, ky * 16 + hh * 8 + 8)
                    for layer in range(2):
                        oz = (0.125, 0.375)[layer] if s == 0 else (-0.375, -0.125)[layer]
                        plane = layer if s == 0 else 18 + layer
                        p_s[f, plane, rows, :] = (
                            (centre + slope_z * oz) + slope_y * iy_offset
                        ) + slope_x * ix_offset

    for k in (0, 16):
        z_face(k, 0)
        z_face(k, 1)

    row_f = iota((ROWS, LANES), 0)
    keep = jnp.where(cx32 == (row_f & 3), 0.25, 0.0)
    odd1, odd2 = (row_f & 1) != 0, (row_f & 2) != 0
    terms = [[[] for _ in range(2)] for _ in range(2)]
    for s in range(2):
        for f in range(5):
            x = fz_s[f, 16 * s]
            x = x + jnp.where(odd1, pltpu.roll(x, 1, 0), pltpu.roll(x, ROWS - 1, 0))
            x = x + jnp.where(odd2, pltpu.roll(x, 2, 0), pltpu.roll(x, ROWS - 2, 0))
            x = x * keep
            terms[0][s].append(x[0:16])
            terms[1][s].append(x[16:32])
    pad = jnp.zeros((48, LANES), F32)
    all_terms = jnp.concatenate(
        [jnp.concatenate(terms[ky][s] + [pad], axis=0) for ky in range(2) for s in range(2)], axis=1
    )
    sum_s[...] = sum(dot(spot, x, 1, 1) for x in parts(all_terms))
    exchange(sum_s, sums_s, sum_send, sum_recv, 1, one)
    sums_s[0:MOST, :] = sum_s[0:MOST, :]

    for k in (1, 15):
        z_face(k, 0)
        z_face(k, 1)

    top = face(*[[w_s[f, 1 : 1 + TILES, 38 + i, :] for f in range(5)] for i in range(4)], 1)
    for f in range(5):
        ft_s[f] = top[f]

    def y_faces(t, c):
        lanes = pl.ds(pl.multiple_of(t * LANES, LANES), LANES)
        for half in range(2):
            first = 6 + 16 * half
            w = [[w_s[f, t + 1, first + i : first + i + 16, :] for f in range(5)] for i in range(4)]
            flux = face(*w, 1)
            for f in range(5):
                fy_s[f, 16 * half : 16 * half + 16, :] = flux[f]
        for f in range(5):
            fy_s[f, ROWS : ROWS + 1, :] = ft_s[f, pl.ds(t, 1), :]
        for f in range(5):
            low, high = fx_s[f, t + 1], fx_s[f, t + 2]
            dx = pltpu.roll(jnp.where(lane_r < 16, high, low), LANES - 16, 1) - low
            dy = fy_s[f, 1 : 1 + ROWS, :] - fy_s[f, 0:ROWS, :]
            out[f, :, lanes] = q_s[f, :, lanes] - DT_DX * (dx + dy)
        return c

    lax.fori_loop(0, TILES, y_faces, 0)

    def finish(n, c):
        f, rb = n // 4, n % 4
        rows = pl.ds(pl.multiple_of(rb * 8, 8), 8)
        z = [fz_s[f, k, rows, :] for k in range(17)]
        tiles = swap_tiles([z[k + 1] - z[k] for k in range(16)])
        for t in range(TILES):
            lanes = slice(t * LANES, (t + 1) * LANES)
            out[f, rows, lanes] = out[f, rows, lanes] - DT_DX * tiles[t]
        return c

    lax.fori_loop(0, 20, finish, 0, unroll=4)

    all_of(sums_s, sum_send, sum_recv, rest).wait()
    total = sum(dot(x, chosen, 0, 0) for x in parts(sums_s[...]))
    for f in range(5):
        for s in range(2):
            register[f, 16 * s : 16 * s + 16, :] = total[
                16 * f : 16 * f + 16, s * LANES : (s + 1) * LANES
            ]


def local(fine_state, coarse_boxes, piece_owner, piece_box):
    members, groups = lax.axis_size("dev"), lax.axis_size("group")
    boxes = coarse_boxes.transpose(1, 0, 2)
    owner = piece_owner.reshape(1, PIECES_DEV)
    box = piece_box.reshape(1, PIECES_DEV)
    vmem = lambda *shape, dtype=F32: pltpu.VMEM(shape, dtype)
    dma = pltpu.SemaphoreType.DMA
    return pl.pallas_call(
        functools.partial(kernel, members, groups),
        out_shape=(
            vmem(*fine_state.shape),
            vmem(5, 32, BOX_DEV),
        ),
        in_specs=[pl.BlockSpec(memory_space=pltpu.HBM)] * 4,
        out_specs=[pl.BlockSpec(memory_space=pltpu.VMEM)] * 2,
        scratch_shapes=[
            vmem(5, ROWS, TILES * LANES),
            vmem(5, TILES + 2, 48, LANES),
            vmem(5, 20, ROWS, LANES),
            vmem(5, TILES + 2, ROWS, LANES),
            vmem(5, 40, LANES),
            vmem(5, TILES, LANES),
            vmem(5, 17, ROWS, LANES),
            vmem(5, BOX_DEV, 512),
            vmem(3, 2 * BOX_DEV, 3 * LANES, dtype=BF16),
            vmem(1, PIECES_DEV, dtype=jnp.int32),
            vmem(1, PIECES_DEV, dtype=jnp.int32),
            vmem(LANES, LANES),
            vmem(LANES, LANES),
            vmem(3, LANES, LANES),
            vmem(3, LANES, LANES),
            vmem(LANES, LANES),
            vmem(LANES, LANES),
            vmem(3, LANES, 4 * LANES),
            vmem(3, 4, 32, LANES),
            vmem(2, 5, ROWS, LANES),
            vmem(2, 5, 2, TILES * LANES),
            dma((4,)),
            dma, dma, dma, dma, dma, dma,
            dma((4,)),
            dma((4,)),
        ],
        compiler_params=pltpu.CompilerParams(
            collective_id=0, has_side_effects=True, vmem_limit_bytes=40 * 1024 * 1024
        ),
    )(*[pltpu.with_memory_space_constraint(x, pltpu.HBM) for x in (fine_state, boxes, owner, box)])


def solution(mesh):
    in_specs = (
        P(None, "group", "dev"),
        P(("group", "dev"), None, None),
        P(("group", "dev"), None),
        P(("group", "dev")),
    )
    out_specs = (P(None, "group", "dev"), P(None, None, ("group", "dev")))
    return jax.shard_map(local, mesh=mesh, in_specs=in_specs, out_specs=out_specs, check_vma=False)
```

```python
import functools

import jax
import jax.numpy as jnp
from jax import lax
from jax.experimental import pallas as pl
from jax.experimental.pallas import tpu as pltpu
from jax.sharding import PartitionSpec as P

BOX_DEV = 128
PIECES_DEV = 32
MOST = 4
GAMMA = 1.4
DT_DX = 0.08
TILES = 16
ROWS = 32
LANES = 128
MESH = pl.DeviceIdType.MESH
F32 = jnp.float32
BF16 = jnp.bfloat16


def iota(shape, axis):
    return lax.broadcasted_iota(jnp.int32, shape, axis)


def minmod(a, b):
    return jnp.maximum(jnp.minimum(a, b), jnp.minimum(jnp.maximum(a, b), 0.0))


def primitives(q):
    r = 1.0 / q[0]
    u, v, w = q[1] * r, q[2] * r, q[3] * r
    p = (GAMMA - 1.0) * (q[4] - 0.5 * (q[1] * u + q[2] * v + q[3] * w))
    return [q[0], u, v, w, p]


def hll(low, up, normal):
    n = 1 + normal
    t1, t2 = [i for i in (1, 2, 3) if i != n]
    rl, ul, pl_ = low[0], low[n], low[4]
    ru, uu, pu = up[0], up[n], up[4]
    ql, qu = GAMMA * pl_, GAMMA * pu
    cl = ql * lax.rsqrt(ql * rl)
    cu = qu * lax.rsqrt(qu * ru)
    slow = jnp.minimum(jnp.minimum(ul - cl, uu - cu), 0.0)
    fast = jnp.maximum(jnp.maximum(ul + cl, uu + cu), 0.0)
    inverse = 1.0 / (fast - slow)
    a = fast * inverse
    b = slow * inverse
    e = slow * a
    aul = a * ul
    buu = b * uu
    wl = aul - e
    wu = e - buu
    ml = rl * wl
    mu = ru * wu
    nl, nu = ml * ul, mu * uu
    v1l, v1u = ml * low[t1], mu * up[t1]
    v2l, v2u = ml * low[t2], mu * up[t2]
    kinetic = (nl * ul + v1l * low[t1] + v2l * low[t2]) + (nu * uu + v1u * up[t1] + v2u * up[t2])
    flux = [None] * 5
    flux[0] = ml + mu
    flux[n] = (nl + nu) + (a * pl_ - b * pu)
    flux[t1] = v1l + v1u
    flux[t2] = v2l + v2u
    flux[4] = 0.5 * kinetic + (pl_ * (2.5 * wl + aul) + pu * (2.5 * wu - buu))
    return flux


def face(before_two, before, here, after, normal):
    low, up = [], []
    for f in range(5):
        d1 = here[f] - before[f]
        low.append(before[f] + 0.5 * minmod(before[f] - before_two[f], d1))
        up.append(here[f] - 0.5 * minmod(d1, after[f] - here[f]))
    return hll(low, up, normal)


def swap_tiles(tiles):
    tiles = list(tiles)
    lane = iota(tiles[0].shape, 1)
    for bit in range(4):
        step = 1 << bit
        odd = (lane & step) != 0
        for t in range(16):
            if t & step:
                continue
            a, b = tiles[t], tiles[t + step]
            tiles[t] = jnp.where(odd, pltpu.roll(b, step, 1), a)
            tiles[t + step] = jnp.where(odd, b, pltpu.roll(a, LANES - step, 1))
    return tiles


def parts(x):
    first = x.astype(BF16)
    rest = x - first.astype(F32)
    second = rest.astype(BF16)
    third = (rest - second.astype(F32)).astype(BF16)
    return first, second, third


def kernel(
    members, groups,
    fine, boxes, owner_in, box_in,
    out, register,
    q_s, w_s, p_s, fx_s, fy_s, ft_s, fz_s, cb_s, u_s, owner_s, box_s,
    ask_s, asked_s, give_s, got_s, sum_s, sums_s, ex_s, se_s, xh_s, yh_s,
    load_sem, ask_send, ask_recv, give_send, give_recv, sum_send, sum_recv, halo_send, halo_recv,
):
    me = lax.axis_index("dev")
    group = lax.axis_index("group")

    load_ids = [
        pltpu.make_async_copy(owner_in, owner_s, load_sem.at[0]),
        pltpu.make_async_copy(box_in, box_s, load_sem.at[1]),
    ]
    load_boxes = pltpu.make_async_copy(boxes, cb_s, load_sem.at[2])
    load_fine = pltpu.make_async_copy(fine, q_s, load_sem.at[3])
    for copy in load_ids:
        copy.start()
    load_boxes.start()
    load_fine.start()

    barrier = pltpu.get_barrier_semaphore()
    north, south = lax.rem(group + 1, groups), lax.rem(group + groups - 1, groups)

    def greet(k, c):
        pl.semaphore_signal(
            barrier, inc=1, device_id=(group, lax.rem(me + k, members)), device_id_type=MESH
        )
        return c

    for y in (north, south):
        pl.semaphore_signal(barrier, inc=1, device_id=(y, me), device_id_type=MESH)
    lax.fori_loop(1, members, greet, 0)

    lane1 = iota((1, LANES), 1)
    row128 = iota((LANES, LANES), 0)
    lane128 = iota((LANES, LANES), 1)
    lane8 = iota((8, LANES), 1)
    row8 = iota((8, LANES), 0)

    for copy in load_ids:
        copy.wait()
    live = lane1 < PIECES_DEV
    fill = jnp.full((1, LANES - PIECES_DEV), -1, jnp.int32)
    owner = jnp.concatenate([owner_s[...], fill], axis=1)
    box = jnp.concatenate([box_s[...], fill], axis=1)
    row32, lane32 = iota((PIECES_DEV, LANES), 0), iota((PIECES_DEV, LANES), 1)
    owner_f = owner.astype(F32)
    owner_all = jnp.broadcast_to(owner_f, (PIECES_DEV, LANES))
    owner_col = jnp.sum(jnp.where(lane32 == row32, owner_all, 0.0), axis=1, keepdims=True)
    same = (jnp.broadcast_to(owner_col, (PIECES_DEV, LANES)) == owner_all) & (row32 < lane32)
    rank = jnp.sum(jnp.where(same, 1.0, 0.0), axis=0, keepdims=True)
    away = owner - me
    away = jnp.where(away < 0, away + members, away)
    slot = jnp.where(live, MOST * away + rank.astype(jnp.int32), -1)
    value = (box + 1 + BOX_DEV * (lane1 & 1)).astype(F32)
    hit = row128 == jnp.broadcast_to(slot, (LANES, LANES))
    asked_value = jnp.sum(
        jnp.where(hit, jnp.broadcast_to(value, (LANES, LANES)), 0.0), axis=1, keepdims=True
    )
    ask_s[...] = jnp.broadcast_to(asked_value, (LANES, LANES))

    load_boxes.wait()

    def table(n, c):
        rows = pl.ds(pl.multiple_of(n * 16, 16), 16)
        lane = iota((16, LANES), 1)
        lo = lane < 64
        t = [[cb_s[f, rows, k * LANES : (k + 1) * LANES] for k in range(4)] for f in range(5)]
        mid = primitives([jnp.where(lo, t[f][1], t[f][2]) for f in range(5)])
        below = primitives([jnp.where(lo, t[f][2], t[f][0]) for f in range(5)])
        above = primitives([jnp.where(lo, t[f][3], t[f][1]) for f in range(5)])
        first_y, first_x = (lane & 32) == 0, (lane & 4) == 0
        packed = []
        for f in range(5):
            m = mid[f]
            sz = minmod(m - pltpu.roll(below[f], 64, 1), pltpu.roll(above[f], 64, 1) - m)
            sy = minmod(m - pltpu.roll(m, 8, 1), pltpu.roll(m, LANES - 8, 1) - m)
            sx = minmod(m - pltpu.roll(m, 1, 1), pltpu.roll(m, LANES - 1, 1) - m)
            packed.append(
                jnp.where(
                    first_y,
                    jnp.where(first_x, pltpu.roll(m, LANES - 18, 1), pltpu.roll(sz, LANES - 14, 1)),
                    jnp.where(first_x, pltpu.roll(sy, 14, 1), pltpu.roll(sx, 18, 1)),
                )
            )
        cx, h, coef, cy = lane >> 5, (lane >> 4) & 1, (lane >> 2) & 3, lane & 3
        source = h * 64 + (coef >> 1) * 32 + cy * 8 + (coef & 1) * 4 + cx
        for pair in range(3):
            a = packed[2 * pair]
            b = packed[2 * pair + 1] if pair < 2 else a
            for side, tile in (
                (0, jnp.where(lo, pltpu.roll(a, 64, 1), b)),
                (1, jnp.where(lo, a, pltpu.roll(b, 64, 1))),
            ):
                moved = jnp.take_along_axis(tile, source, axis=1)
                where = pl.ds(pl.multiple_of(side * BOX_DEV + n * 16, 16), 16)
                for i, x in enumerate(parts(moved)):
                    u_s[i, where, pair * LANES : (pair + 1) * LANES] = x
        return c

    lax.fori_loop(0, BOX_DEV // 32, table, 0, unroll=4)

    pl.semaphore_wait(barrier, members + 1)

    def exchange(buffer, landed, send, recv, sign, part):
        def copy(k):
            return pltpu.make_async_remote_copy(
                src_ref=part(buffer, k),
                dst_ref=part(landed, k),
                send_sem=send,
                recv_sem=recv,
                device_id=(group, lax.rem(me + sign * k + members, members)),
                device_id_type=MESH,
            )

        def start(k, c):
            copy(k).start()
            return c

        lax.fori_loop(1, members, start, 0)

    def all_of(landed, send, recv, part):
        whole = part(landed)
        return pltpu.make_async_remote_copy(
            src_ref=whole, dst_ref=whole, send_sem=send, recv_sem=recv,
            device_id=(group, lax.rem(me + 1, members)), device_id_type=MESH,
        )

    one = lambda ref, k: ref.at[pl.ds(k * MOST, MOST)]
    one3 = lambda ref, k: ref.at[:, pl.ds(k * MOST, MOST)]
    rest = lambda ref: ref.at[pl.ds(MOST, (members - 1) * MOST)]
    rest3 = lambda ref: ref.at[:, pl.ds(MOST, (members - 1) * MOST)]

    exchange(ask_s, asked_s, ask_send, ask_recv, 1, one)
    asked_s[0:MOST, :] = ask_s[0:MOST, :]

    right, left = lax.rem(me + 1, members), lax.rem(me + members - 1, members)
    last = fine.shape[2] - LANES
    halos = [
        (fine.at[:, :, pl.ds(last, LANES)], xh_s.at[0], (group, right)),
        (fine.at[:, :, pl.ds(0, LANES)], xh_s.at[1], (group, left)),
        (fine.at[:, pl.ds(ROWS - 2, 2)], yh_s.at[0], (north, me)),
        (fine.at[:, pl.ds(0, 2)], yh_s.at[1], (south, me)),
    ]
    halo_copies = [
        pltpu.make_async_remote_copy(
            src_ref=src, dst_ref=dst, send_sem=halo_send.at[i], recv_sem=halo_recv.at[i],
            device_id=target, device_id_type=MESH,
        )
        for i, (src, dst, target) in enumerate(halos)
    ]
    for copy in halo_copies:
        copy.start()

    spots = []
    for ky in range(2):
        v = slot if ky == 0 else pltpu.roll(slot, LANES - 16, 1)
        v = jnp.where(lane1 < 16, v, 0)
        for step in (16, 32, 64):
            v = v + pltpu.roll(v, step, 1)
        odd = (lane1 & 1) != 0
        spots.append(jnp.where(odd, pltpu.roll(v, 1, 1), v))
        spots.append(jnp.where(odd, v, pltpu.roll(v, LANES - 1, 1)))
    spot = jnp.concatenate(
        [
            jnp.where(row128 == jnp.broadcast_to(s, (LANES, LANES)), 1.0, 0.0).astype(BF16)
            for s in spots
        ],
        axis=1,
    )

    lax.fori_loop(BOX_DEV // 32, BOX_DEV // 16, table, 0, unroll=4)

    load_fine.wait()

    def to_primitive(t, c):
        lanes = pl.ds(pl.multiple_of(t * LANES, LANES), LANES)
        w = primitives([q_s[f, :, lanes] for f in range(5)])
        for f in range(5):
            w_s[f, t + 1, 8 : 8 + ROWS, :] = w[f]
        return c

    lax.fori_loop(0, TILES, to_primitive, 0)

    def pack(n, c):
        f, rb = n // 4, n % 4
        rows = pl.ds(pl.multiple_of(8 + rb * 8, 8), 8)
        tiles = swap_tiles([w_s[f, 1 + t, rows, :] for t in range(TILES)])
        for z in range(16):
            p_s[f, 2 + z, pl.ds(pl.multiple_of(rb * 8, 8), 8), :] = tiles[z]
        return c

    lax.fori_loop(0, 20, pack, 0, unroll=4)

    all_of(asked_s, ask_send, ask_recv, rest).wait()
    asked = asked_s[...]
    lane_f = lane128.astype(F32)
    chosen = jnp.concatenate(
        [
            jnp.where(asked == lane_f + (1.0 + BOX_DEV * side), 1.0, 0.0).astype(BF16)
            for side in range(2)
        ],
        axis=1,
    )

    def dot(a, b, da, db):
        return lax.dot_general(a, b, (((da,), (db,)), ((), ())), preferred_element_type=F32)

    give = sum(dot(chosen, u_s[i], 1, 0) for i in range(3))
    for pair in range(3):
        give_s[pair] = give[:, pair * LANES : (pair + 1) * LANES]
    exchange(give_s, got_s, give_send, give_recv, -1, one3)
    got_s[:, 0:MOST, :] = give_s[:, 0:MOST, :]

    def z_face(k, half):
        rows = slice(16 * half, 16 * half + 16)
        w = [[p_s[f, k + i, rows, :] for f in range(5)] for i in range(4)]
        flux = face(*w, 2)
        for f in range(5):
            fz_s[f, k, rows, :] = flux[f]

    def z_inner(k, c):
        z_face(k, 0)
        z_face(k, 1)
        return c

    lax.fori_loop(2, 15, z_inner, 0)

    for copy in halo_copies:
        copy.wait()
    lane_r = iota((ROWS, LANES), 1)
    x_low = primitives([xh_s[0, f] for f in range(5)])
    x_high = primitives([xh_s[1, f] for f in range(5)])
    is_first = jnp.full((ROWS, LANES), me, jnp.int32) == 0
    is_last = jnp.full((ROWS, LANES), me, jnp.int32) == members - 1
    inner = slice(8, 8 + ROWS)
    for f in range(5):
        begin, end = w_s[f, 1, inner, :], w_s[f, TILES, inner, :]
        low_edge = jnp.where(lane_r < 112, pltpu.roll(begin, 96, 1), pltpu.roll(begin, 112, 1))
        high_edge = jnp.where(lane_r < 16, pltpu.roll(end, 16, 1), pltpu.roll(end, 32, 1))
        w_s[f, 0, inner, :] = jnp.where(is_first, low_edge, x_low[f])
        w_s[f, TILES + 1, inner, :] = jnp.where(is_last, high_edge, x_high[f])

    def y_halo(t, c):
        lanes = pl.ds(pl.multiple_of(t * LANES, LANES), LANES)
        low = primitives([yh_s[0, f, :, lanes] for f in range(5)])
        high = primitives([yh_s[1, f, :, lanes] for f in range(5)])
        for f in range(5):
            w_s[f, t + 1, 6:8, :] = low[f]
            w_s[f, t + 1, 8 + ROWS : 10 + ROWS, :] = high[f]
        return c

    lax.fori_loop(0, TILES, y_halo, 0)

    lane_h = iota((16, LANES), 1)

    def x_faces(t, c):
        after_tile = jnp.minimum(t + 1, TILES + 1)
        for half in range(2):
            rows = slice(8 + 16 * half, 24 + 16 * half)
            w = [[], [], [], []]
            for f in range(5):
                left_tile, tile, right_tile = w_s[f, t - 1, rows, :], w_s[f, t, rows, :], w_s[f, after_tile, rows, :]
                w[0].append(pltpu.roll(jnp.where(lane_h >= 96, left_tile, tile), 32, 1))
                w[1].append(pltpu.roll(jnp.where(lane_h >= 112, left_tile, tile), 16, 1))
                w[2].append(tile)
                w[3].append(pltpu.roll(jnp.where(lane_h < 16, right_tile, tile), LANES - 16, 1))
            flux = face(*w, 0)
            for f in range(5):
                fx_s[f, t, 16 * half : 16 * half + 16, :] = flux[f]
        return c

    lax.fori_loop(1, TILES + 2, x_faces, 0)

    all_of(got_s, give_send, give_recv, rest3).wait()
    for pair in range(3):
        got = parts(got_s[pair])
        ex_s[pair] = sum(dot(x, spot, 0, 0) for x in got)
    t8, i8 = lane8 & 15, lane8 >> 4
    cx8 = 2 * (t8 & 1) + (i8 >> 2)
    ix_offset = ((i8 & 3).astype(F32) + 0.5) * 0.25 - 0.5
    iy_offset = ((row8 & 3).astype(F32) + 0.5) * 0.25 - 0.5
    cx32 = 2 * (lane_r & 1) + (lane_r >> 6)
    for pair in range(3):
        for kys in range(4):
            lanes = slice(kys * LANES, (kys + 1) * LANES)
            x = [ex_s[pair, 32 * cx : 32 * cx + 32, lanes] for cx in range(4)]
            se_s[pair, kys] = jnp.where(
                cx32 < 2, jnp.where(cx32 == 0, x[0], x[1]), jnp.where(cx32 == 2, x[2], x[3])
            )
    for f in range(5):
        pair, h = f // 2, f % 2
        for ky in range(2):
            for s in range(2):
                kys = 2 * ky + s
                for hh in range(2):
                    def coefficient(q):
                        r = h * 16 + q * 4 + 2 * hh
                        return jnp.where(
                            row8 < 4,
                            jnp.broadcast_to(se_s[pair, kys, r : r + 1, :], (8, LANES)),
                            jnp.broadcast_to(se_s[pair, kys, r + 1 : r + 2, :], (8, LANES)),
                        )

                    centre, slope_z = coefficient(0), coefficient(1)
                    slope_y, slope_x = coefficient(2), coefficient(3)
                    rows = slice(ky * 16 + hh * 8, ky * 16 + hh * 8 + 8)
                    for layer in range(2):
                        oz = (0.125, 0.375)[layer] if s == 0 else (-0.375, -0.125)[layer]
                        plane = layer if s == 0 else 18 + layer
                        p_s[f, plane, rows, :] = (
                            (centre + slope_z * oz) + slope_y * iy_offset
                        ) + slope_x * ix_offset

    for k in (0, 16):
        z_face(k, 0)
        z_face(k, 1)

    row_f = iota((ROWS, LANES), 0)
    keep = jnp.where(cx32 == (row_f & 3), 0.25, 0.0)
    odd1, odd2 = (row_f & 1) != 0, (row_f & 2) != 0
    terms = [[[] for _ in range(2)] for _ in range(2)]
    for s in range(2):
        for f in range(5):
            x = fz_s[f, 16 * s]
            x = x + jnp.where(odd1, pltpu.roll(x, 1, 0), pltpu.roll(x, ROWS - 1, 0))
            x = x + jnp.where(odd2, pltpu.roll(x, 2, 0), pltpu.roll(x, ROWS - 2, 0))
            x = x * keep
            terms[0][s].append(x[0:16])
            terms[1][s].append(x[16:32])
    pad = jnp.zeros((48, LANES), F32)
    all_terms = jnp.concatenate(
        [jnp.concatenate(terms[ky][s] + [pad], axis=0) for ky in range(2) for s in range(2)], axis=1
    )
    sum_s[...] = sum(dot(spot, x, 1, 1) for x in parts(all_terms))
    exchange(sum_s, sums_s, sum_send, sum_recv, 1, one)
    sums_s[0:MOST, :] = sum_s[0:MOST, :]

    for k in (1, 15):
        z_face(k, 0)
        z_face(k, 1)

    top = face(*[[w_s[f, 1 : 1 + TILES, 38 + i, :] for f in range(5)] for i in range(4)], 1)
    for f in range(5):
        ft_s[f] = top[f]

    def y_faces(t, c):
        lanes = pl.ds(pl.multiple_of(t * LANES, LANES), LANES)
        for half in range(2):
            first = 6 + 16 * half
            w = [[w_s[f, t + 1, first + i : first + i + 16, :] for f in range(5)] for i in range(4)]
            flux = face(*w, 1)
            for f in range(5):
                fy_s[f, 16 * half : 16 * half + 16, :] = flux[f]
        for f in range(5):
            fy_s[f, ROWS : ROWS + 1, :] = ft_s[f, pl.ds(t, 1), :]
        for f in range(5):
            low, high = fx_s[f, t + 1], fx_s[f, t + 2]
            dx = pltpu.roll(jnp.where(lane_r < 16, high, low), LANES - 16, 1) - low
            dy = fy_s[f, 1 : 1 + ROWS, :] - fy_s[f, 0:ROWS, :]
            out[f, :, lanes] = q_s[f, :, lanes] - DT_DX * (dx + dy)
        return c

    lax.fori_loop(0, TILES, y_faces, 0)

    def finish(n, c):
        f, rb = n // 4, n % 4
        rows = pl.ds(pl.multiple_of(rb * 8, 8), 8)
        z = [fz_s[f, k, rows, :] for k in range(17)]
        tiles = swap_tiles([z[k + 1] - z[k] for k in range(16)])
        for t in range(TILES):
            lanes = slice(t * LANES, (t + 1) * LANES)
            out[f, rows, lanes] = out[f, rows, lanes] - DT_DX * tiles[t]
        return c

    lax.fori_loop(0, 20, finish, 0, unroll=4)

    all_of(sums_s, sum_send, sum_recv, rest).wait()
    total = sum(dot(x, chosen, 0, 0) for x in parts(sums_s[...]))
    for f in range(5):
        for s in range(2):
            register[f, 16 * s : 16 * s + 16, :] = total[
                16 * f : 16 * f + 16, s * LANES : (s + 1) * LANES
            ]


def local(fine_state, coarse_boxes, piece_owner, piece_box):
    members, groups = lax.axis_size("dev"), lax.axis_size("group")
    boxes = coarse_boxes.transpose(1, 0, 2)
    owner = piece_owner.reshape(1, PIECES_DEV)
    box = piece_box.reshape(1, PIECES_DEV)
    vmem = lambda *shape, dtype=F32: pltpu.VMEM(shape, dtype)
    dma = pltpu.SemaphoreType.DMA
    return pl.pallas_call(
        functools.partial(kernel, members, groups),
        out_shape=(
            vmem(*fine_state.shape),
            vmem(5, 32, BOX_DEV),
        ),
        in_specs=[pl.BlockSpec(memory_space=pltpu.HBM)] * 4,
        out_specs=[pl.BlockSpec(memory_space=pltpu.VMEM)] * 2,
        scratch_shapes=[
            vmem(5, ROWS, TILES * LANES),
            vmem(5, TILES + 2, 48, LANES),
            vmem(5, 20, ROWS, LANES),
            vmem(5, TILES + 2, ROWS, LANES),
            vmem(5, 40, LANES),
            vmem(5, TILES, LANES),
            vmem(5, 17, ROWS, LANES),
            vmem(5, BOX_DEV, 512),
            vmem(3, 2 * BOX_DEV, 3 * LANES, dtype=BF16),
            vmem(1, PIECES_DEV, dtype=jnp.int32),
            vmem(1, PIECES_DEV, dtype=jnp.int32),
            vmem(LANES, LANES),
            vmem(LANES, LANES),
            vmem(3, LANES, LANES),
            vmem(3, LANES, LANES),
            vmem(LANES, LANES),
            vmem(LANES, LANES),
            vmem(3, LANES, 4 * LANES),
            vmem(3, 4, 32, LANES),
            vmem(2, 5, ROWS, LANES),
            vmem(2, 5, 2, TILES * LANES),
            dma((4,)),
            dma, dma, dma, dma, dma, dma,
            dma((4,)),
            dma((4,)),
        ],
        compiler_params=pltpu.CompilerParams(
            collective_id=0, has_side_effects=True, vmem_limit_bytes=40 * 1024 * 1024
        ),
    )(*[pltpu.with_memory_space_constraint(x, pltpu.HBM) for x in (fine_state, boxes, owner, box)])


def solution(mesh):
    in_specs = (
        P(None, "group", "dev"),
        P(("group", "dev"), None, None),
        P(("group", "dev"), None),
        P(("group", "dev")),
    )
    out_specs = (P(None, "group", "dev"), P(None, None, ("group", "dev")))
    return jax.shard_map(local, mesh=mesh, in_specs=in_specs, out_specs=out_specs, check_vma=False)
```

```python
import functools

import jax
import jax.numpy as jnp
from jax import lax
from jax.experimental import pallas as pl
from jax.experimental.pallas import tpu as pltpu
from jax.sharding import PartitionSpec as P

BOX_DEV = 128
PIECES_DEV = 32
MOST = 4
GAMMA = 1.4
DT_DX = 0.08
TILES = 16
ROWS = 32
LANES = 128
MESH = pl.DeviceIdType.MESH
F32 = jnp.float32
BF16 = jnp.bfloat16


def iota(shape, axis):
    return lax.broadcasted_iota(jnp.int32, shape, axis)


def minmod(a, b):
    return jnp.maximum(jnp.minimum(a, b), jnp.minimum(jnp.maximum(a, b), 0.0))


def primitives(q):
    r = 1.0 / q[0]
    u, v, w = q[1] * r, q[2] * r, q[3] * r
    p = (GAMMA - 1.0) * (q[4] - 0.5 * (q[1] * u + q[2] * v + q[3] * w))
    return [q[0], u, v, w, p]


def hll(low, up, normal):
    n = 1 + normal
    t1, t2 = [i for i in (1, 2, 3) if i != n]
    rl, ul, pl_ = low[0], low[n], low[4]
    ru, uu, pu = up[0], up[n], up[4]
    ql, qu = GAMMA * pl_, GAMMA * pu
    cl = ql * lax.rsqrt(ql * rl)
    cu = qu * lax.rsqrt(qu * ru)
    slow = jnp.minimum(jnp.minimum(ul - cl, uu - cu), 0.0)
    fast = jnp.maximum(jnp.maximum(ul + cl, uu + cu), 0.0)
    inverse = 1.0 / (fast - slow)
    a = fast * inverse
    b = slow * inverse
    e = slow * a
    aul = a * ul
    buu = b * uu
    wl = aul - e
    wu = e - buu
    ml = rl * wl
    mu = ru * wu
    nl, nu = ml * ul, mu * uu
    v1l, v1u = ml * low[t1], mu * up[t1]
    v2l, v2u = ml * low[t2], mu * up[t2]
    kinetic = (nl * ul + v1l * low[t1] + v2l * low[t2]) + (nu * uu + v1u * up[t1] + v2u * up[t2])
    flux = [None] * 5
    flux[0] = ml + mu
    flux[n] = (nl + nu) + (a * pl_ - b * pu)
    flux[t1] = v1l + v1u
    flux[t2] = v2l + v2u
    flux[4] = 0.5 * kinetic + (pl_ * (2.5 * wl + aul) + pu * (2.5 * wu - buu))
    return flux


def face(before_two, before, here, after, normal):
    low, up = [], []
    for f in range(5):
        d1 = here[f] - before[f]
        low.append(before[f] + 0.5 * minmod(before[f] - before_two[f], d1))
        up.append(here[f] - 0.5 * minmod(d1, after[f] - here[f]))
    return hll(low, up, normal)


def swap_tiles(tiles):
    tiles = list(tiles)
    lane = iota(tiles[0].shape, 1)
    for bit in range(4):
        step = 1 << bit
        odd = (lane & step) != 0
        for t in range(16):
            if t & step:
                continue
            a, b = tiles[t], tiles[t + step]
            tiles[t] = jnp.where(odd, pltpu.roll(b, step, 1), a)
            tiles[t + step] = jnp.where(odd, b, pltpu.roll(a, LANES - step, 1))
    return tiles


def parts(x):
    first = x.astype(BF16)
    rest = x - first.astype(F32)
    second = rest.astype(BF16)
    third = (rest - second.astype(F32)).astype(BF16)
    return first, second, third


def kernel(
    members, groups,
    fine, boxes, owner_in, box_in,
    out, register,
    q_s, w_s, p_s, fx_s, fy_s, ft_s, fz_s, cb_s, u_s, owner_s, box_s,
    ask_s, asked_s, give_s, got_s, sum_s, sums_s, ex_s, se_s, xh_s, yh_s,
    load_sem, ask_send, ask_recv, give_send, give_recv, sum_send, sum_recv, halo_send, halo_recv,
):
    me = lax.axis_index("dev")
    group = lax.axis_index("group")

    load_ids = [
        pltpu.make_async_copy(owner_in, owner_s, load_sem.at[0]),
        pltpu.make_async_copy(box_in, box_s, load_sem.at[1]),
    ]
    load_boxes = pltpu.make_async_copy(boxes, cb_s, load_sem.at[2])
    load_fine = pltpu.make_async_copy(fine, q_s, load_sem.at[3])
    for copy in load_ids:
        copy.start()
    load_boxes.start()
    load_fine.start()

    barrier = pltpu.get_barrier_semaphore()
    north, south = lax.rem(group + 1, groups), lax.rem(group + groups - 1, groups)

    def greet(k, c):
        pl.semaphore_signal(
            barrier, inc=1, device_id=(group, lax.rem(me + k, members)), device_id_type=MESH
        )
        return c

    for y in (north, south):
        pl.semaphore_signal(barrier, inc=1, device_id=(y, me), device_id_type=MESH)
    lax.fori_loop(1, members, greet, 0)

    lane1 = iota((1, LANES), 1)
    row128 = iota((LANES, LANES), 0)
    lane128 = iota((LANES, LANES), 1)
    lane8 = iota((8, LANES), 1)
    row8 = iota((8, LANES), 0)

    for copy in load_ids:
        copy.wait()
    live = lane1 < PIECES_DEV
    fill = jnp.full((1, LANES - PIECES_DEV), -1, jnp.int32)
    owner = jnp.concatenate([owner_s[...], fill], axis=1)
    box = jnp.concatenate([box_s[...], fill], axis=1)
    row32, lane32 = iota((PIECES_DEV, LANES), 0), iota((PIECES_DEV, LANES), 1)
    owner_f = owner.astype(F32)
    owner_all = jnp.broadcast_to(owner_f, (PIECES_DEV, LANES))
    owner_col = jnp.sum(jnp.where(lane32 == row32, owner_all, 0.0), axis=1, keepdims=True)
    same = (jnp.broadcast_to(owner_col, (PIECES_DEV, LANES)) == owner_all) & (row32 < lane32)
    rank = jnp.sum(jnp.where(same, 1.0, 0.0), axis=0, keepdims=True)
    away = owner - me
    away = jnp.where(away < 0, away + members, away)
    slot = jnp.where(live, MOST * away + rank.astype(jnp.int32), -1)
    value = (box + 1 + BOX_DEV * (lane1 & 1)).astype(F32)
    hit = row128 == jnp.broadcast_to(slot, (LANES, LANES))
    asked_value = jnp.sum(
        jnp.where(hit, jnp.broadcast_to(value, (LANES, LANES)), 0.0), axis=1, keepdims=True
    )
    ask_s[...] = jnp.broadcast_to(asked_value, (LANES, LANES))

    load_boxes.wait()

    def table(n, c):
        rows = pl.ds(pl.multiple_of(n * 16, 16), 16)
        lane = iota((16, LANES), 1)
        lo = lane < 64
        t = [[cb_s[f, rows, k * LANES : (k + 1) * LANES] for k in range(4)] for f in range(5)]
        mid = primitives([jnp.where(lo, t[f][1], t[f][2]) for f in range(5)])
        below = primitives([jnp.where(lo, t[f][2], t[f][0]) for f in range(5)])
        above = primitives([jnp.where(lo, t[f][3], t[f][1]) for f in range(5)])
        first_y, first_x = (lane & 32) == 0, (lane & 4) == 0
        packed = []
        for f in range(5):
            m = mid[f]
            sz = minmod(m - pltpu.roll(below[f], 64, 1), pltpu.roll(above[f], 64, 1) - m)
            sy = minmod(m - pltpu.roll(m, 8, 1), pltpu.roll(m, LANES - 8, 1) - m)
            sx = minmod(m - pltpu.roll(m, 1, 1), pltpu.roll(m, LANES - 1, 1) - m)
            packed.append(
                jnp.where(
                    first_y,
                    jnp.where(first_x, pltpu.roll(m, LANES - 18, 1), pltpu.roll(sz, LANES - 14, 1)),
                    jnp.where(first_x, pltpu.roll(sy, 14, 1), pltpu.roll(sx, 18, 1)),
                )
            )
        cx, h, coef, cy = lane >> 5, (lane >> 4) & 1, (lane >> 2) & 3, lane & 3
        source = h * 64 + (coef >> 1) * 32 + cy * 8 + (coef & 1) * 4 + cx
        for pair in range(3):
            a = packed[2 * pair]
            b = packed[2 * pair + 1] if pair < 2 else a
            for side, tile in (
                (0, jnp.where(lo, pltpu.roll(a, 64, 1), b)),
                (1, jnp.where(lo, a, pltpu.roll(b, 64, 1))),
            ):
                moved = jnp.take_along_axis(tile, source, axis=1)
                where = pl.ds(pl.multiple_of(side * BOX_DEV + n * 16, 16), 16)
                for i, x in enumerate(parts(moved)):
                    u_s[i, where, pair * LANES : (pair + 1) * LANES] = x
        return c

    lax.fori_loop(0, BOX_DEV // 32, table, 0, unroll=4)

    load_fine.wait()

    def to_primitive(t, c):
        lanes = pl.ds(pl.multiple_of(t * LANES, LANES), LANES)
        w = primitives([q_s[f, :, lanes] for f in range(5)])
        for f in range(5):
            w_s[f, t + 1, 8 : 8 + ROWS, :] = w[f]
        return c

    lax.fori_loop(0, TILES, to_primitive, 0)

    pl.semaphore_wait(barrier, members + 1)

    def exchange(buffer, landed, send, recv, sign, part):
        def copy(k):
            return pltpu.make_async_remote_copy(
                src_ref=part(buffer, k),
                dst_ref=part(landed, k),
                send_sem=send,
                recv_sem=recv,
                device_id=(group, lax.rem(me + sign * k + members, members)),
                device_id_type=MESH,
            )

        def start(k, c):
            copy(k).start()
            return c

        lax.fori_loop(1, members, start, 0)

    def all_of(landed, send, recv, part):
        whole = part(landed)
        return pltpu.make_async_remote_copy(
            src_ref=whole, dst_ref=whole, send_sem=send, recv_sem=recv,
            device_id=(group, lax.rem(me + 1, members)), device_id_type=MESH,
        )

    one = lambda ref, k: ref.at[pl.ds(k * MOST, MOST)]
    one3 = lambda ref, k: ref.at[:, pl.ds(k * MOST, MOST)]
    rest = lambda ref: ref.at[pl.ds(MOST, (members - 1) * MOST)]
    rest3 = lambda ref: ref.at[:, pl.ds(MOST, (members - 1) * MOST)]

    exchange(ask_s, asked_s, ask_send, ask_recv, 1, one)
    asked_s[0:MOST, :] = ask_s[0:MOST, :]

    right, left = lax.rem(me + 1, members), lax.rem(me + members - 1, members)
    last = fine.shape[2] - LANES
    halos = [
        (fine.at[:, :, pl.ds(last, LANES)], xh_s.at[0], (group, right)),
        (fine.at[:, :, pl.ds(0, LANES)], xh_s.at[1], (group, left)),
        (fine.at[:, pl.ds(ROWS - 2, 2)], yh_s.at[0], (north, me)),
        (fine.at[:, pl.ds(0, 2)], yh_s.at[1], (south, me)),
    ]
    halo_copies = [
        pltpu.make_async_remote_copy(
            src_ref=src, dst_ref=dst, send_sem=halo_send.at[i], recv_sem=halo_recv.at[i],
            device_id=target, device_id_type=MESH,
        )
        for i, (src, dst, target) in enumerate(halos)
    ]
    for copy in halo_copies:
        copy.start()

    spots = []
    for ky in range(2):
        v = slot if ky == 0 else pltpu.roll(slot, LANES - 16, 1)
        v = jnp.where(lane1 < 16, v, 0)
        for step in (16, 32, 64):
            v = v + pltpu.roll(v, step, 1)
        odd = (lane1 & 1) != 0
        spots.append(jnp.where(odd, pltpu.roll(v, 1, 1), v))
        spots.append(jnp.where(odd, v, pltpu.roll(v, LANES - 1, 1)))
    spot = jnp.concatenate(
        [
            jnp.where(row128 == jnp.broadcast_to(s, (LANES, LANES)), 1.0, 0.0).astype(BF16)
            for s in spots
        ],
        axis=1,
    )

    lax.fori_loop(BOX_DEV // 32, BOX_DEV // 16, table, 0, unroll=4)


    def pack(n, c):
        f, rb = n // 4, n % 4
        rows = pl.ds(pl.multiple_of(8 + rb * 8, 8), 8)
        tiles = swap_tiles([w_s[f, 1 + t, rows, :] for t in range(TILES)])
        for z in range(16):
            p_s[f, 2 + z, pl.ds(pl.multiple_of(rb * 8, 8), 8), :] = tiles[z]
        return c

    lax.fori_loop(0, 20, pack, 0, unroll=4)

    asks = all_of(asked_s, ask_send, ask_recv, rest)
    asks.wait_recv()
    asked = asked_s[...]
    lane_f = lane128.astype(F32)
    chosen = jnp.concatenate(
        [
            jnp.where(asked == lane_f + (1.0 + BOX_DEV * side), 1.0, 0.0).astype(BF16)
            for side in range(2)
        ],
        axis=1,
    )

    def dot(a, b, da, db):
        return lax.dot_general(a, b, (((da,), (db,)), ((), ())), preferred_element_type=F32)

    give = sum(dot(chosen, u_s[i], 1, 0) for i in range(3))
    for pair in range(3):
        give_s[pair] = give[:, pair * LANES : (pair + 1) * LANES]
    exchange(give_s, got_s, give_send, give_recv, -1, one3)
    got_s[:, 0:MOST, :] = give_s[:, 0:MOST, :]

    def z_face(k, half):
        rows = slice(16 * half, 16 * half + 16)
        w = [[p_s[f, k + i, rows, :] for f in range(5)] for i in range(4)]
        flux = face(*w, 2)
        for f in range(5):
            fz_s[f, k, rows, :] = flux[f]

    def z_inner(k, c):
        z_face(k, 0)
        z_face(k, 1)
        return c

    lax.fori_loop(2, 15, z_inner, 0)

    for copy in halo_copies:
        copy.wait_recv()
    lane_r = iota((ROWS, LANES), 1)
    x_low = primitives([xh_s[0, f] for f in range(5)])
    x_high = primitives([xh_s[1, f] for f in range(5)])
    is_first = jnp.full((ROWS, LANES), me, jnp.int32) == 0
    is_last = jnp.full((ROWS, LANES), me, jnp.int32) == members - 1
    inner = slice(8, 8 + ROWS)
    for f in range(5):
        begin, end = w_s[f, 1, inner, :], w_s[f, TILES, inner, :]
        low_edge = jnp.where(lane_r < 112, pltpu.roll(begin, 96, 1), pltpu.roll(begin, 112, 1))
        high_edge = jnp.where(lane_r < 16, pltpu.roll(end, 16, 1), pltpu.roll(end, 32, 1))
        w_s[f, 0, inner, :] = jnp.where(is_first, low_edge, x_low[f])
        w_s[f, TILES + 1, inner, :] = jnp.where(is_last, high_edge, x_high[f])

    def y_halo(t, c):
        lanes = pl.ds(pl.multiple_of(t * LANES, LANES), LANES)
        low = primitives([yh_s[0, f, :, lanes] for f in range(5)])
        high = primitives([yh_s[1, f, :, lanes] for f in range(5)])
        for f in range(5):
            w_s[f, t + 1, 6:8, :] = low[f]
            w_s[f, t + 1, 8 + ROWS : 10 + ROWS, :] = high[f]
        return c

    lax.fori_loop(0, TILES, y_halo, 0)

    lane_h = iota((16, LANES), 1)

    def x_faces(t, c):
        after_tile = jnp.minimum(t + 1, TILES + 1)
        for half in range(2):
            rows = slice(8 + 16 * half, 24 + 16 * half)
            w = [[], [], [], []]
            for f in range(5):
                left_tile, tile, right_tile = w_s[f, t - 1, rows, :], w_s[f, t, rows, :], w_s[f, after_tile, rows, :]
                w[0].append(pltpu.roll(jnp.where(lane_h >= 96, left_tile, tile), 32, 1))
                w[1].append(pltpu.roll(jnp.where(lane_h >= 112, left_tile, tile), 16, 1))
                w[2].append(tile)
                w[3].append(pltpu.roll(jnp.where(lane_h < 16, right_tile, tile), LANES - 16, 1))
            flux = face(*w, 0)
            for f in range(5):
                fx_s[f, t, 16 * half : 16 * half + 16, :] = flux[f]
        return c

    lax.fori_loop(1, TILES + 2, x_faces, 0)

    gifts = all_of(got_s, give_send, give_recv, rest3)
    gifts.wait_recv()
    for pair in range(3):
        got = parts(got_s[pair])
        ex_s[pair] = sum(dot(x, spot, 0, 0) for x in got)
    t8, i8 = lane8 & 15, lane8 >> 4
    cx8 = 2 * (t8 & 1) + (i8 >> 2)
    ix_offset = ((i8 & 3).astype(F32) + 0.5) * 0.25 - 0.5
    iy_offset = ((row8 & 3).astype(F32) + 0.5) * 0.25 - 0.5
    cx32 = 2 * (lane_r & 1) + (lane_r >> 6)
    for pair in range(3):
        for kys in range(4):
            lanes = slice(kys * LANES, (kys + 1) * LANES)
            x = [ex_s[pair, 32 * cx : 32 * cx + 32, lanes] for cx in range(4)]
            se_s[pair, kys] = jnp.where(
                cx32 < 2, jnp.where(cx32 == 0, x[0], x[1]), jnp.where(cx32 == 2, x[2], x[3])
            )
    for f in range(5):
        pair, h = f // 2, f % 2
        for ky in range(2):
            for s in range(2):
                kys = 2 * ky + s
                for hh in range(2):
                    def coefficient(q):
                        r = h * 16 + q * 4 + 2 * hh
                        return jnp.where(
                            row8 < 4,
                            jnp.broadcast_to(se_s[pair, kys, r : r + 1, :], (8, LANES)),
                            jnp.broadcast_to(se_s[pair, kys, r + 1 : r + 2, :], (8, LANES)),
                        )

                    centre, slope_z = coefficient(0), coefficient(1)
                    slope_y, slope_x = coefficient(2), coefficient(3)
                    rows = slice(ky * 16 + hh * 8, ky * 16 + hh * 8 + 8)
                    for layer in range(2):
                        oz = (0.125, 0.375)[layer] if s == 0 else (-0.375, -0.125)[layer]
                        plane = layer if s == 0 else 18 + layer
                        p_s[f, plane, rows, :] = (
                            (centre + slope_z * oz) + slope_y * iy_offset
                        ) + slope_x * ix_offset

    for k in (0, 16):
        z_face(k, 0)
        z_face(k, 1)

    row_f = iota((ROWS, LANES), 0)
    keep = jnp.where(cx32 == (row_f & 3), 0.25, 0.0)
    odd1, odd2 = (row_f & 1) != 0, (row_f & 2) != 0
    terms = [[[] for _ in range(2)] for _ in range(2)]
    for s in range(2):
        for f in range(5):
            x = fz_s[f, 16 * s]
            x = x + jnp.where(odd1, pltpu.roll(x, 1, 0), pltpu.roll(x, ROWS - 1, 0))
            x = x + jnp.where(odd2, pltpu.roll(x, 2, 0), pltpu.roll(x, ROWS - 2, 0))
            x = x * keep
            terms[0][s].append(x[0:16])
            terms[1][s].append(x[16:32])
    pad = jnp.zeros((48, LANES), F32)
    all_terms = jnp.concatenate(
        [jnp.concatenate(terms[ky][s] + [pad], axis=0) for ky in range(2) for s in range(2)], axis=1
    )
    sum_s[...] = sum(dot(spot, x, 1, 1) for x in parts(all_terms))
    exchange(sum_s, sums_s, sum_send, sum_recv, 1, one)
    sums_s[0:MOST, :] = sum_s[0:MOST, :]

    for k in (1, 15):
        z_face(k, 0)
        z_face(k, 1)

    top = face(*[[w_s[f, 1 : 1 + TILES, 38 + i, :] for f in range(5)] for i in range(4)], 1)
    for f in range(5):
        ft_s[f] = top[f]

    def y_faces(t, c):
        lanes = pl.ds(pl.multiple_of(t * LANES, LANES), LANES)
        for half in range(2):
            first = 6 + 16 * half
            w = [[w_s[f, t + 1, first + i : first + i + 16, :] for f in range(5)] for i in range(4)]
            flux = face(*w, 1)
            for f in range(5):
                fy_s[f, 16 * half : 16 * half + 16, :] = flux[f]
        for f in range(5):
            fy_s[f, ROWS : ROWS + 1, :] = ft_s[f, pl.ds(t, 1), :]
        for f in range(5):
            low, high = fx_s[f, t + 1], fx_s[f, t + 2]
            dx = pltpu.roll(jnp.where(lane_r < 16, high, low), LANES - 16, 1) - low
            dy = fy_s[f, 1 : 1 + ROWS, :] - fy_s[f, 0:ROWS, :]
            out[f, :, lanes] = q_s[f, :, lanes] - DT_DX * (dx + dy)
        return c

    lax.fori_loop(0, TILES, y_faces, 0, unroll=2)

    def finish(n, c):
        f, rb = n // 4, n % 4
        rows = pl.ds(pl.multiple_of(rb * 8, 8), 8)
        z = [fz_s[f, k, rows, :] for k in range(17)]
        tiles = swap_tiles([z[k + 1] - z[k] for k in range(16)])
        for t in range(TILES):
            lanes = slice(t * LANES, (t + 1) * LANES)
            out[f, rows, lanes] = out[f, rows, lanes] - DT_DX * tiles[t]
        return c

    lax.fori_loop(0, 20, finish, 0, unroll=4)

    totals = all_of(sums_s, sum_send, sum_recv, rest)
    totals.wait_recv()
    total = sum(dot(x, chosen, 0, 0) for x in parts(sums_s[...]))
    for f in range(5):
        for s in range(2):
            register[f, 16 * s : 16 * s + 16, :] = total[
                16 * f : 16 * f + 16, s * LANES : (s + 1) * LANES
            ]
    for copy in (asks, gifts, totals, *halo_copies):
        copy.wait_send()


def local(fine_state, coarse_boxes, piece_owner, piece_box):
    members, groups = lax.axis_size("dev"), lax.axis_size("group")
    boxes = coarse_boxes.transpose(1, 0, 2)
    owner = piece_owner.reshape(1, PIECES_DEV)
    box = piece_box.reshape(1, PIECES_DEV)
    vmem = lambda *shape, dtype=F32: pltpu.VMEM(shape, dtype)
    dma = pltpu.SemaphoreType.DMA
    return pl.pallas_call(
        functools.partial(kernel, members, groups),
        out_shape=(
            vmem(*fine_state.shape),
            vmem(5, 32, BOX_DEV),
        ),
        in_specs=[pl.BlockSpec(memory_space=pltpu.HBM)] * 4,
        out_specs=[pl.BlockSpec(memory_space=pltpu.VMEM)] * 2,
        scratch_shapes=[
            vmem(5, ROWS, TILES * LANES),
            vmem(5, TILES + 2, 48, LANES),
            vmem(5, 20, ROWS, LANES),
            vmem(5, TILES + 2, ROWS, LANES),
            vmem(5, 40, LANES),
            vmem(5, TILES, LANES),
            vmem(5, 17, ROWS, LANES),
            vmem(5, BOX_DEV, 512),
            vmem(3, 2 * BOX_DEV, 3 * LANES, dtype=BF16),
            vmem(1, PIECES_DEV, dtype=jnp.int32),
            vmem(1, PIECES_DEV, dtype=jnp.int32),
            vmem(LANES, LANES),
            vmem(LANES, LANES),
            vmem(3, LANES, LANES),
            vmem(3, LANES, LANES),
            vmem(LANES, LANES),
            vmem(LANES, LANES),
            vmem(3, LANES, 4 * LANES),
            vmem(3, 4, 32, LANES),
            vmem(2, 5, ROWS, LANES),
            vmem(2, 5, 2, TILES * LANES),
            dma((4,)),
            dma, dma, dma, dma, dma, dma,
            dma((4,)),
            dma((4,)),
        ],
        compiler_params=pltpu.CompilerParams(
            collective_id=0, has_side_effects=True, vmem_limit_bytes=40 * 1024 * 1024
        ),
    )(*[pltpu.with_memory_space_constraint(x, pltpu.HBM) for x in (fine_state, boxes, owner, box)])


def solution(mesh):
    in_specs = (
        P(None, "group", "dev"),
        P(("group", "dev"), None, None),
        P(("group", "dev"), None),
        P(("group", "dev")),
    )
    out_specs = (P(None, "group", "dev"), P(None, None, ("group", "dev")))
    return jax.shard_map(local, mesh=mesh, in_specs=in_specs, out_specs=out_specs, check_vma=False)
```
